32 devices in a mesh: dp: 8 (over z, x), tensor: 4 (over y, core).
Axes of the slice: x: 2, y: 2, z: 4, core: 2. Of those that a mesh axis runs over, the one named last changes fastest.
Arguments:
- tokens: bfloat16 [32, 1024, 512], P(('dp', 'tensor')), may hold values from -6 to 6
- clip_ids: int32 [32, 1024], P('dp'), may hold values from 0 to 15, never falling along the last dimension, each value on 1 to 128 neighbouring positions
- ln1_gain: float32 [512], replicated, may hold values from 0.5 to 1.5
- ln1_bias: float32 [512], replicated, may hold values from -3 to 3
- query_key_value_weight: bfloat16 [512, 3, 512], P(None, None, 'tensor'), may hold values from -0.25 to 0.25
- projection_weight: bfloat16 [512, 512], P('tensor'), may hold values from -0.75 to 0.75
- attention_output_bias: float32 [512], replicated, may hold values from -3 to 3
- ln2_gain: float32 [512], replicated, may hold values from 0.5 to 1.5
- ln2_bias: float32 [512], replicated, may hold values from -3 to 3
- up_weight: bfloat16 [512, 2048], P(None, 'tensor'), may hold values from -0.25 to 0.25
- mlp_up_bias: float32 [2048], P('tensor'), may hold values from -3 to 3
- down_weight: bfloat16 [2048, 512], P('tensor'), may hold values from -0.1875 to 0.1875
- mlp_down_bias: float32 [512], replicated, may hold values from -3 to 3
- grad_output: bfloat16 [32, 1024, 512], P(('dp', 'tensor')), may hold values from -6 to 6
Outputs:
- output: bfloat16 [32, 1024, 512], P(('dp', 'tensor'))
- grad_tokens: bfloat16 [32, 1024, 512], P(('dp', 'tensor'))
- g_ln1_gain: float32 [512], P(('dp', 'tensor'))
- g_ln1_bias: float32 [512], P(('dp', 'tensor'))
- query_key_value_gradient: float32 [512, 3, 512], P('dp', None, 'tensor')
- projection_weight_gradient: float32 [512, 512], P('tensor', 'dp')
- g_proj_bias: float32 [512], P(('dp', 'tensor'))
- g_ln2_gain: float32 [512], P(('dp', 'tensor'))
- g_ln2_bias: float32 [512], P(('dp', 'tensor'))
- up_weight_gradient: float32 [512, 2048], P('dp', 'tensor')
- g_up_bias: float32 [4, 512], P('tensor', 'dp')
- down_weight_gradient: float32 [2048, 512], P('tensor', 'dp')
- g_down_bias: float32 [512], P(('dp', 'tensor'))
The draws below stay inside these ranges and needn't reach their ends.
Inputs may be any that keep to these rules, and one draw needn't show every extreme that they name: `clip_ids`: within a sequence clip numbers never fall from one time step to the next; each clip holds 1 to 128 time steps, and some clip exactly 128.
All inputs are finite; a program needn't handle non-finite values.
Results may differ from the reference program's by a relative error of at most 0.019.
Values may be sent and summed in bfloat16 or wider, within the bound.
A program may use at most 192 MiB of HBM per device.

```python
import math
import jax
import jax.numpy as jnp
import numpy as np
from jax import lax

D = 512
HEADS = 8
HD = 64
FF = 2048
SEQ = 1024
SEQS_DEV = 1
CLIPS = 16
CLIP_MOST = 128
SEQS = 32
N_TENSOR = 4


def levels(rng, extent, shards, smallest, largest):
    factor_of, own = 1.0, jax.random.fold_in(rng, 6)
    for axis_at, shards_of in shards:
        steps = jnp.exp(jax.random.uniform(jax.random.fold_in(own, axis_at), (shards_of,), jnp.float32, smallest / len(shards), largest / len(shards)))
        factor_of = factor_of * jnp.repeat(steps, extent[axis_at] // shards_of).reshape([-1 if axis == axis_at else 1 for axis in range(len(extent))])
    return factor_of


def length_profile(number_of, total, most, skew):
    loads = [(1 << 20) // math.isqrt(rank ** skew) + 1 for rank in range(2, number_of + 1)]
    surplus, given = total - most - (number_of - 1), [1] * (number_of - 1)
    while surplus > 0:
        candidates = [i for i in range(number_of - 1) if given[i] < most]
        whole, left = sum([loads[i] for i in candidates]), surplus
        for i in candidates:
            addition = min(most - given[i], max(1, left * loads[i] // whole), surplus)
            given[i] = given[i] + addition
            surplus = surplus - addition
    return np.array([most] + given)


def uneven(own_key, count, total, most, lean):
    if count == 2:
        one = jax.random.randint(own_key, (), max(1, total - most), min(most, total - 1) + 1)
        return jnp.stack([one, total - one])
    lengths = jnp.asarray(length_profile(count, total, most, lean), jnp.int32)
    pairs = (count - 1) // 2
    giver, receiver = lengths[1:1 + 2 * pairs:2], lengths[2:2 + 2 * pairs:2]
    margin = jnp.minimum(giver - 1, most - receiver)
    passed = jax.random.randint(jax.random.fold_in(own_key, 1), (pairs,), 0, 1 << 20) % (margin + 1)
    lengths = lengths.at[1:1 + 2 * pairs:2].set(giver - passed).at[2:2 + 2 * pairs:2].set(receiver + passed)
    return lengths[jax.random.permutation(jax.random.fold_in(own_key, 2), count)]


def normal_values(stream_key, dims, scale, bound, split=(), held_as=jnp.bfloat16):
    drawn = scale * jax.random.normal(stream_key, dims, jnp.float32)
    if split:
        drawn = drawn * levels(stream_key, dims, split, -0.22, 0.18)
    return jnp.clip(drawn, -bound, bound).astype(held_as)


def setup_inputs(seed: int = 0) -> dict:
    seeds = jax.random.split(jax.random.key(seed), 15)
    return {
        "tokens": normal_values(seeds[0], (SEQS, SEQ, D), 1.0, 6.0, ((0, 32),)),
        "clip_ids": jax.vmap(lambda own: jnp.searchsorted(jnp.cumsum(uneven(own, CLIPS, SEQ, CLIP_MOST, 1)), jnp.arange(SEQ), side="right"))(jax.random.split(seeds[1], SEQS)).reshape((SEQS, SEQ)).astype(jnp.int32),
        "ln1_gain": jnp.clip(1.0 + 0.1 * jax.random.normal(seeds[2], (D,), jnp.float32), 0.5, 1.5),
        "ln1_bias": normal_values(seeds[3], (D,), 0.3, 3.0, (), jnp.float32),
        "query_key_value_weight": normal_values(seeds[4], (D, 3, D), D ** -0.5, 0.25, ((2, 4),)),
        "projection_weight": normal_values(seeds[5], (D, D), (D // 8) ** -0.5, 0.75, ((0, 4),)),
        "attention_output_bias": normal_values(seeds[6], (D,), 0.3, 3.0, (), jnp.float32),
        "ln2_gain": jnp.clip(1.0 + 0.1 * jax.random.normal(seeds[7], (D,), jnp.float32), 0.5, 1.5),
        "ln2_bias": normal_values(seeds[8], (D,), 0.3, 3.0, (), jnp.float32),
        "up_weight": normal_values(seeds[9], (D, FF), D ** -0.5, 0.25, ((1, 4),)),
        "mlp_up_bias": normal_values(seeds[10], (FF,), 0.5, 3.0, ((0, 4),), jnp.float32),
        "down_weight": normal_values(seeds[11], (FF, D), (FF // 2) ** -0.5, 0.1875, ((0, 4),)),
        "mlp_down_bias": normal_values(seeds[12], (D,), 0.3, 3.0, (), jnp.float32),
        "grad_output": normal_values(seeds[13], (SEQS, SEQ, D), 1.0, 6.0, ((0, 32),)),
    }


@jax.custom_vjp
def low_precision_rows(v):
    return lax.optimization_barrier(v.astype(jnp.bfloat16)).astype(jnp.float32)

@jax.custom_vjp
def low_precision_backward(v):
    return v

def low_keep(v):
    return (low_precision_rows(v), None)

def low_pass(kept, grad):
    return (grad,)

def back_keep(v):
    return (v, None)

def back_low(kept, grad):
    return (low_precision_rows(grad),)
low_precision_rows.defvjp(low_keep, low_pass)
low_precision_backward.defvjp(back_keep, back_low)
epsilon = 1e-05
best_choice_found = lax.Precision.HIGHEST

def layer_norm(values, gain, shift):
    centre = values - lax.optimization_barrier(jnp.mean(values, axis=-1, keepdims=True))
    spread = lax.optimization_barrier(jnp.mean(centre * centre, axis=-1, keepdims=True))
    return centre * lax.rsqrt(spread + epsilon) * gain + shift

def attend(pieces):
    query, keys, vals, clip_row = pieces
    length = query.shape[0]
    scale = query.shape[-1] ** (-0.5)
    scores = low_precision_backward(jnp.einsum('qhd,khd->hqk', query, keys, precision=best_choice_found) * scale)
    place = jnp.arange(length)
    allowed = (place[None, :] <= place[:, None]) & (clip_row[:, None] == clip_row[None, :])
    scores = jnp.where(allowed[None], scores, -1e+30)
    peak = lax.optimization_barrier(jnp.max(scores, axis=-1, keepdims=True))
    expo = jnp.exp(scores - peak)
    probs = low_precision_rows(expo / lax.optimization_barrier(jnp.sum(expo, axis=-1, keepdims=True)))
    return jnp.einsum('hqk,khd->qhd', probs, vals, precision=best_choice_found)

def layer(tokens, clip_ids, ln1_gain, ln1_bias, query_key_value_weight, projection_weight, attention_output_bias, ln2_gain, ln2_bias, up_weight, mlp_up_bias, down_weight, mlp_down_bias):
    seqs, length, width = tokens.shape
    first_normalized = low_precision_rows(layer_norm(tokens, ln1_gain, ln1_bias))
    query_key_value_rows = low_precision_backward(low_precision_rows(jnp.einsum('tre,eub->trub', first_normalized, query_key_value_weight, precision=best_choice_found)))
    query_key_value_rows = query_key_value_rows.reshape(seqs, length, 3, HEADS, HD)
    mixed_heads_output = lax.map(jax.checkpoint(attend), (query_key_value_rows[:, :, 0], query_key_value_rows[:, :, 1], query_key_value_rows[:, :, 2], clip_ids))
    mixed_heads_output = low_precision_backward(low_precision_rows(mixed_heads_output.reshape(seqs, length, width)))
    hidden_activation = tokens + low_precision_backward(jnp.einsum('bne,eo->bno', mixed_heads_output, projection_weight, precision=best_choice_found)) + attention_output_bias
    second_normalized = low_precision_rows(layer_norm(hidden_activation, ln2_gain, ln2_bias))
    upper_half_rows = low_precision_backward(jnp.einsum('wih,hm->wim', second_normalized, up_weight, precision=best_choice_found) + mlp_up_bias)
    active_rows_now = low_precision_rows(jax.nn.gelu(upper_half_rows, approximate=False))
    return hidden_activation + jnp.einsum('bne,eo->bno', active_rows_now, down_weight, precision=best_choice_found) + mlp_down_bias

def reference(tokens, clip_ids, ln1_gain, ln1_bias, query_key_value_weight, projection_weight, attention_output_bias, ln2_gain, ln2_bias, up_weight, mlp_up_bias, down_weight, mlp_down_bias, grad_output):
    params = tuple((p.astype(jnp.float32) for p in (ln1_gain, ln1_bias, query_key_value_weight, projection_weight, attention_output_bias, ln2_gain, ln2_bias, up_weight, mlp_up_bias, down_weight, mlp_down_bias)))
    groups = tokens.shape[0] // SEQS_DEV

    def shaped(values):
        return values.reshape((groups, SEQS_DEV) + values.shape[1:])

    def one_group(totals, pieces):
        block, clip_block, grad_block = pieces

        def run(block_values, *weights):
            return layer(block_values, clip_block, *weights)
        result, pull = jax.vjp(run, block.astype(jnp.float32), *params)
        grads = pull(grad_block.astype(jnp.float32))
        totals = tuple((a + b for a, b in zip(totals, grads[1:])))
        return (totals, (result.astype(jnp.bfloat16), grads[0].astype(jnp.bfloat16)))
    zeros = tuple((jnp.zeros_like(p) for p in params))
    totals, (outputs, grad_in) = lax.scan(one_group, zeros, (shaped(tokens), shaped(clip_ids), shaped(grad_output)))
    g_ln1_gain, g_ln1_bias, query_key_value_gradient, projection_weight_gradient, g_proj_bias, g_ln2_gain, g_ln2_bias, up_weight_gradient, g_up_bias, down_weight_gradient, g_down_bias = totals
    return (outputs.reshape(tokens.shape), grad_in.reshape(tokens.shape), g_ln1_gain, g_ln1_bias, query_key_value_gradient, projection_weight_gradient, g_proj_bias, g_ln2_gain, g_ln2_bias, up_weight_gradient, g_up_bias.reshape(N_TENSOR, -1), down_weight_gradient, g_down_bias)
```

```python
import functools
import math

import jax
import jax.numpy as jnp
from jax import lax
from jax.experimental import pallas as pl
from jax.experimental.pallas import tpu as pltpu
from jax.sharding import PartitionSpec as P

HD = 64
CORES = 2
WIDE = 2
BF = jnp.bfloat16
F32 = jnp.float32
MESH = pl.DeviceIdType.MESH


epsilon = 1e-05


def layer_norm(values, gain, shift):
    centre = values - jnp.mean(values, axis=-1, keepdims=True)
    spread = jnp.mean(centre * centre, axis=-1, keepdims=True)
    return centre * lax.rsqrt(spread + epsilon) * gain + shift


def gelu_exact(values):
    return jax.nn.gelu(values, approximate=False)


def visible(clip_row, start, count):
    length = clip_row.shape[0]
    query_pos = start + jnp.arange(count)
    key_pos = jnp.arange(length)
    query_clip = clip_row[start : start + count]
    return (key_pos[None, :] <= query_pos[:, None]) & (query_clip[:, None] == clip_row[None, :])


def block_scores(query, keys, clip_row, start, block):
    scale = query.shape[-1] ** (-0.5)
    allowed = visible(clip_row, start, block)
    scores = (
        jnp.einsum(
            "qhd,khd->hqk", query[start : start + block], keys, preferred_element_type=jnp.float32
        )
        * scale
    )
    return (jnp.where(allowed[None], scores, -1e30), allowed)


def attend_sequence(pieces):
    query, keys, vals, clip_row = pieces
    length = query.shape[0]
    block = min(512, length)
    outs = []
    sums = []
    for start in range(0, length, block):
        scores, allowed = block_scores(query, keys, clip_row, start, block)
        peak = jnp.max(scores, axis=-1, keepdims=True)
        expo = jnp.exp(scores - peak)
        total = jnp.sum(expo, axis=-1, keepdims=True)
        probs = (expo / total).astype(jnp.bfloat16)
        outs.append(jnp.einsum("hqk,khd->qhd", probs, vals, preferred_element_type=jnp.float32))
        sums.append((peak + jnp.log(total))[..., 0])
    return (jnp.concatenate(outs, 0), jnp.concatenate(sums, 1))


def attend_back(pieces):
    query, keys, vals, clip_row, lse, grad_mixed = pieces
    length = query.shape[0]
    block = min(512, length)
    scale = query.shape[-1] ** (-0.5)
    grad_keys = jnp.zeros(keys.shape, jnp.float32)
    grad_vals = jnp.zeros(vals.shape, jnp.float32)
    query_parts = []
    for start in range(0, length, block):
        scores, allowed = block_scores(query, keys, clip_row, start, block)
        probs_f = jnp.where(
            allowed[None], jnp.exp(scores - lse[:, start : start + block, None]), 0.0
        )
        probs = probs_f.astype(jnp.bfloat16)
        grad_block = grad_mixed[start : start + block]
        dprobs = jnp.einsum("qhd,khd->hqk", grad_block, vals, preferred_element_type=jnp.float32)
        grad_vals = grad_vals + jnp.einsum(
            "hqk,qhd->khd", probs, grad_block, preferred_element_type=jnp.float32
        )
        inner = jnp.sum(probs_f * dprobs, axis=-1, keepdims=True)
        dscores = (probs_f * (dprobs - inner)).astype(jnp.bfloat16)
        query_parts.append(
            jnp.einsum("hqk,khd->qhd", dscores, keys, preferred_element_type=jnp.float32) * scale
        )
        grad_keys = (
            grad_keys
            + jnp.einsum(
                "hqk,qhd->khd",
                dscores,
                query[start : start + block],
                preferred_element_type=jnp.float32,
            )
            * scale
        )
    return (jnp.concatenate(query_parts, 0), grad_keys, grad_vals)


def on_device(
    tokens,
    clip_ids,
    ln1_gain,
    ln1_bias,
    query_key_value_weight,
    projection_weight,
    attention_output_bias,
    ln2_gain,
    ln2_bias,
    up_weight,
    mlp_up_bias,
    down_weight,
    mlp_down_bias,
    grad_output,
):
    head_size = HD
    local_width = query_key_value_weight.shape[2]
    local_heads = local_width // head_size
    tok_f = tokens.astype(jnp.float32)
    first_normalized = layer_norm(tok_f, ln1_gain, ln1_bias).astype(jnp.bfloat16)
    first_normalized_every = lax.all_gather(first_normalized, "tensor", axis=0, tiled=True)
    seqs = first_normalized_every.shape[0]
    length = first_normalized_every.shape[1]
    query_key_value_rows = jnp.einsum(
        "tre,eub->trub",
        first_normalized_every,
        query_key_value_weight,
        preferred_element_type=jnp.float32,
    ).astype(jnp.bfloat16)
    query_key_value_rows = query_key_value_rows.reshape(seqs, length, 3, local_heads, head_size)
    query = query_key_value_rows[:, :, 0]
    keys = query_key_value_rows[:, :, 1]
    vals = query_key_value_rows[:, :, 2]
    mixed_heads_output, lse = lax.map(attend_sequence, (query, keys, vals, clip_ids))
    mixed_heads_lowered = mixed_heads_output.astype(jnp.bfloat16).reshape(seqs, length, local_width)
    attention_piece = jnp.einsum(
        "bne,eo->bno", mixed_heads_lowered, projection_weight, preferred_element_type=jnp.float32
    )
    attn_rows = lax.psum_scatter(
        attention_piece.astype(jnp.bfloat16), "tensor", scatter_dimension=0, tiled=True
    ).astype(jnp.float32)
    hidden_activation = tok_f + attn_rows + attention_output_bias
    second_normalized = layer_norm(hidden_activation, ln2_gain, ln2_bias).astype(jnp.bfloat16)
    second_normalized_every = lax.all_gather(second_normalized, "tensor", axis=0, tiled=True)
    upper_half_rows = (
        jnp.einsum(
            "wih,hm->wim", second_normalized_every, up_weight, preferred_element_type=jnp.float32
        )
        + mlp_up_bias
    )
    active_rows_now = gelu_exact(upper_half_rows).astype(jnp.bfloat16)
    perceptron_piece = jnp.einsum(
        "bne,eo->bno", active_rows_now, down_weight, preferred_element_type=jnp.float32
    )
    mlp_rows = lax.psum_scatter(
        perceptron_piece.astype(jnp.bfloat16), "tensor", scatter_dimension=0, tiled=True
    ).astype(jnp.float32)
    output = (hidden_activation + mlp_rows + mlp_down_bias).astype(jnp.bfloat16)
    gradient_every_row = lax.all_gather(grad_output, "tensor", axis=0, tiled=True)
    down_weight_gradient = jnp.einsum(
        "egz,egb->zb", active_rows_now, gradient_every_row, preferred_element_type=jnp.float32
    )
    gradient_active_rows = jnp.einsum(
        "etk,ok->eto", gradient_every_row, down_weight, preferred_element_type=jnp.float32
    )
    gradient_upper_half = jax.vjp(gelu_exact, upper_half_rows)[1](gradient_active_rows)[0].astype(
        jnp.bfloat16
    )
    g_up_bias = jnp.sum(gradient_upper_half, axis=(0, 1), dtype=jnp.float32)
    up_weight_gradient = jnp.einsum(
        "kjy,kjt->yt",
        second_normalized_every,
        gradient_upper_half,
        preferred_element_type=jnp.float32,
    )
    grad_normed2_part = jnp.einsum(
        "hwm,bm->hwb", gradient_upper_half, up_weight, preferred_element_type=jnp.float32
    )
    grad_normed2 = lax.psum_scatter(
        grad_normed2_part.astype(jnp.bfloat16), "tensor", scatter_dimension=0, tiled=True
    ).astype(jnp.float32)
    grad_hidden_ln, g_ln2_gain, g_ln2_bias = jax.vjp(
        layer_norm, hidden_activation, ln2_gain, ln2_bias
    )[1](grad_normed2)
    grad_f = grad_output.astype(jnp.float32)
    grad_hidden = grad_f + grad_hidden_ln
    g_down_bias = jnp.sum(grad_f, axis=(0, 1))
    g_proj_bias = jnp.sum(grad_hidden, axis=(0, 1))
    branch_low = grad_hidden.astype(jnp.bfloat16)
    branch_every_row = lax.all_gather(branch_low, "tensor", axis=0, tiled=True)
    projection_weight_gradient = jnp.einsum(
        "egz,egb->zb", mixed_heads_lowered, branch_every_row, preferred_element_type=jnp.float32
    )
    grad_mixed = jnp.einsum(
        "etk,ok->eto", branch_every_row, projection_weight, preferred_element_type=jnp.float32
    ).astype(jnp.bfloat16)
    grad_mixed = grad_mixed.reshape(seqs, length, local_heads, head_size)
    grad_query, grad_keys, grad_vals = lax.map(
        attend_back, (query, keys, vals, clip_ids, lse, grad_mixed)
    )
    gradient_query_key_value = (
        jnp.stack((grad_query, grad_keys, grad_vals), axis=2)
        .astype(jnp.bfloat16)
        .reshape(seqs, length, 3, local_width)
    )
    query_key_value_gradient = jnp.einsum(
        "zny,znqj->yqj",
        first_normalized_every,
        gradient_query_key_value,
        preferred_element_type=jnp.float32,
    )
    grad_normed_part = jnp.einsum(
        "kegu,hgu->keh",
        gradient_query_key_value,
        query_key_value_weight,
        preferred_element_type=jnp.float32,
    )
    grad_normed = lax.psum_scatter(
        grad_normed_part.astype(jnp.bfloat16), "tensor", scatter_dimension=0, tiled=True
    ).astype(jnp.float32)
    grad_tok_ln, g_ln1_gain, g_ln1_bias = jax.vjp(layer_norm, tok_f, ln1_gain, ln1_bias)[1](
        grad_normed
    )
    grad_tokens = (grad_hidden + grad_tok_ln).astype(jnp.bfloat16)
    g_qkv_s, g_proj_s, g_up_s, g_up_bias_s, g_down_s = (
        lax.psum_scatter(
            query_key_value_gradient.astype(jnp.bfloat16), "dp", scatter_dimension=0, tiled=True
        ).astype(jnp.float32),
        lax.psum_scatter(
            projection_weight_gradient.astype(jnp.bfloat16), "dp", scatter_dimension=1, tiled=True
        ).astype(jnp.float32),
        lax.psum_scatter(
            up_weight_gradient.astype(jnp.bfloat16), "dp", scatter_dimension=0, tiled=True
        ).astype(jnp.float32),
        lax.psum_scatter(
            g_up_bias[None].astype(jnp.bfloat16), "dp", scatter_dimension=1, tiled=True
        ).astype(jnp.float32),
        lax.psum_scatter(
            down_weight_gradient.astype(jnp.bfloat16), "dp", scatter_dimension=1, tiled=True
        ).astype(jnp.float32),
    )
    v_ln1_gain, v_ln1_bias, v_proj_bias, v_ln2_gain, v_ln2_bias, v_down_bias = (
        lax.psum_scatter(g_ln1_gain, ("dp", "tensor"), scatter_dimension=0, tiled=True),
        lax.psum_scatter(g_ln1_bias, ("dp", "tensor"), scatter_dimension=0, tiled=True),
        lax.psum_scatter(g_proj_bias, ("dp", "tensor"), scatter_dimension=0, tiled=True),
        lax.psum_scatter(g_ln2_gain, ("dp", "tensor"), scatter_dimension=0, tiled=True),
        lax.psum_scatter(g_ln2_bias, ("dp", "tensor"), scatter_dimension=0, tiled=True),
        lax.psum_scatter(g_down_bias, ("dp", "tensor"), scatter_dimension=0, tiled=True),
    )
    return (
        output,
        grad_tokens,
        v_ln1_gain,
        v_ln1_bias,
        g_qkv_s,
        g_proj_s,
        v_proj_bias,
        v_ln2_gain,
        v_ln2_bias,
        g_up_s,
        g_up_bias_s,
        g_down_s,
        v_down_bias,
    )


BLOCK = 128
ROWS = 256


def mm(left, right):
    return lax.dot_general(left, right, (((1,), (0,)), ((), ())), preferred_element_type=F32)


def mm_nt(left, right):
    return lax.dot_general(left, right, (((1,), (1,)), ((), ())), preferred_element_type=F32)


def normal_parts(u):
    bell = jnp.exp2(u * u * (-0.5 * math.log2(math.e)))
    base = 1.0 + jnp.abs(u) * (0.3275911 * math.sqrt(0.5))
    t = pl.reciprocal(base, approx=True)
    t = t * (2.0 - base * t)
    poly = 0.5 * 1.061405429
    poly = poly * t - 0.5 * 1.453152027
    poly = poly * t + 0.5 * 1.421413741
    poly = poly * t - 0.5 * 0.284496736
    poly = poly * t + 0.5 * 0.254829592
    half = poly * t * bell
    cdf = jnp.where(u >= 0.0, 1.0 - half, half)
    return cdf, u * bell * (1.0 / math.sqrt(2.0 * math.pi))


def by_eight(values):
    return jnp.sum(values.reshape(-1, 8, values.shape[-1]), axis=0)


class Copies:
    def __init__(self, send, recv):
        self.send, self.recv, self.made, self.started = send, recv, {}, []

    def describe(self, name, src, dst, device):
        at = self.made.setdefault(name, len(self.made))
        return pltpu.make_async_remote_copy(
            src_ref=src,
            dst_ref=dst,
            send_sem=self.send.at[at],
            recv_sem=self.recv.at[at],
            device_id=device,
            device_id_type=MESH,
        )

    def start(self, name, src, dst, device):
        copy = self.describe(name, src, dst, device)
        copy.start()
        self.started.append(copy)

    def arrived(self, name, dst, device):
        self.describe(name, dst, dst, device).wait_recv()

    def drain(self):
        for copy in self.started:
            copy.wait_send()


def layer_kernel(
    sizes,
    tok_h,
    dy_h,
    clip_ref,
    vecs_ref,
    bu_ref,
    wq_h,
    wp_h,
    wu_h,
    wd_h,
    out_h,
    gtok_h,
    gm_ref,
    gq_ref,
    gv_ref,
    tok,
    dy,
    dy_t,
    wq,
    wp,
    wu,
    wd,
    bu,
    n1,
    n1_t,
    stats,
    qs,
    ks,
    vs,
    ks_t,
    vs_t,
    bias,
    probs,
    mixed,
    hidden,
    n2,
    n2_t,
    out_acc,
    dn2_acc,
    act,
    dup,
    dmixed,
    dtri,
    carry,
    vec_acc,
    bup_acc,
    vec_mine,
    vec_t,
    vec_sum,
    vec_dp,
    m_own,
    m_core,
    m_x,
    m_y,
    m_z,
    q_own,
    q_core,
    q_x,
    q_y,
    q_z,
    out_b,
    gtok_b,
    local_sem,
    send_sem,
    recv_sem,
):
    n_t, n_dp, rows, width, heads_w, hidden_w = sizes
    n_y, n_x, n_z = n_t // CORES, WIDE, n_dp // WIDE
    blocks = rows // BLOCK
    d, t = lax.axis_index("dp"), lax.axis_index("tensor")
    y, c = t // CORES, lax.rem(t, CORES)
    z, x = d // WIDE, lax.rem(d, WIDE)

    def t_peer(dy_, dc_):
        return (d, lax.rem(y + dy_, n_y) * CORES + lax.rem(c + dc_, CORES))

    def x_peer(k):
        return (z * WIDE + lax.rem(x + k, n_x), t)

    def z_peer(k):
        return (lax.rem(z + k, n_z) * WIDE + x, t)

    peers = [t_peer(s // CORES, s % CORES) for s in range(1, n_t)]
    peers += [(lax.rem(d + k, n_dp), t) for k in range(1, n_dp)]
    core = t_peer(0, 1)

    barrier = pltpu.get_barrier_semaphore()
    for peer in peers:
        pl.semaphore_signal(barrier, inc=1, device_id=peer, device_id_type=MESH)

    def local(src, dst, at):
        copy = pltpu.make_async_copy(src, dst, local_sem.at[at])
        copy.start()
        return copy

    load_tok = local(tok_h, tok, 0)
    load_wq = local(wq_h, wq.at[0], 1)
    load_wp = local(wp_h, wp.at[0], 2)
    load_dy = local(dy_h, dy, 3)
    load_wu = local(wu_h, wu.at[0], 4)
    load_wd = local(wd_h, wd.at[0], 5)
    bu[0] = jnp.broadcast_to(bu_ref[...], bu.shape[1:])
    pl.semaphore_wait(barrier, len(peers))

    copies = Copies(send_sem, recv_sem)

    full = {"wq": (wq_h, wq), "wp": (wp_h, wp), "wu": (wu_h, wu), "wd": (wd_h, wd)}

    def piece(ref, which):
        part = ref.shape[0] // n_x
        return ref.at[pl.ds(pl.multiple_of(which * part, part), part)]

    def gather_send(name):
        src, dst = full[name]
        for k in range(1, n_y):
            copies.start(
                (name, "y", k), piece(src, x), piece(dst.at[CORES * k], x), t_peer(n_y - k, 0)
            )
        copies.start((name, "core", 0), src, dst.at[1], core)

    def gather_first(name):
        _, dst = full[name]
        for k in range(1, n_y):
            mine = piece(dst.at[CORES * k], x)
            copies.arrived((name, "y", k), mine, core)
            for j in range(1, n_x):
                copies.start((name, "x", k, j), mine, mine, x_peer(j))
            copies.start((name, "core", k, 0), mine, piece(dst.at[CORES * k + 1], x), core)

    def gather_second(name):
        _, dst = full[name]
        for k in range(1, n_y):
            for j in range(1, n_x):
                which = lax.rem(x + n_x - j, n_x)
                got = piece(dst.at[CORES * k], which)
                copies.arrived((name, "x", k, j), got, core)
                copies.start(
                    (name, "core", k, j), got, piece(dst.at[CORES * k + 1], which), core
                )

    def gather_wait(name, s):
        _, dst = full[name]
        if s == 1:
            copies.arrived((name, "core", 0), dst.at[1], core)
        elif s % CORES == 1:
            for j in range(n_x):
                which = lax.rem(x + n_x - j, n_x)
                copies.arrived((name, "core", s // CORES, j), piece(dst.at[s], which), core)

    gather_send("wq")
    for s in range(1, n_t):
        copies.start(
            ("bu", s),
            bu.at[0],
            bu.at[s],
            t_peer((n_y - s // CORES) % n_y, (CORES - s % CORES) % CORES),
        )

    ln1_gain, ln1_bias = vecs_ref[0:1, :], vecs_ref[1:2, :]
    proj_bias = vecs_ref[2:3, :]
    ln2_gain, ln2_bias = vecs_ref[3:4, :], vecs_ref[4:5, :]
    down_bias = vecs_ref[5:6, :]
    vec_acc[...] = jnp.zeros_like(vec_acc)
    bup_acc[...] = jnp.zeros_like(bup_acc)

    clip = clip_ref[pl.ds(t, 1), :].astype(F32)
    key_at = lax.broadcasted_iota(jnp.int32, (BLOCK, BLOCK), 0)
    query_at = lax.broadcasted_iota(jnp.int32, (BLOCK, BLOCK), 1)
    before = jnp.full((BLOCK, BLOCK), -1.0, F32)
    for i in range(blocks):
        row = clip[:, i * BLOCK : (i + 1) * BLOCK]
        ids = jnp.broadcast_to(row, (BLOCK, BLOCK))
        down = ids.T
        bias[i, 0:BLOCK, :] = jnp.where(before == ids, 0.0, -1e30)
        bias[i, BLOCK:, :] = jnp.where((down == ids) & (key_at <= query_at), 0.0, -1e30)
        before = down

    for s in range(n_t):
        ks[s, 0:BLOCK, :] = jnp.zeros((BLOCK, heads_w), BF)
        vs[s, 0:BLOCK, :] = jnp.zeros((BLOCK, heads_w), BF)
        ks_t[s, :, 0:BLOCK] = jnp.zeros((heads_w, BLOCK), BF)
        vs_t[s, :, 0:BLOCK] = jnp.zeros((heads_w, BLOCK), BF)

    def at(i, size, offset=0):
        return pl.ds(pl.multiple_of(i * size + offset, math.gcd(size, offset) if offset else size), size)

    load_tok.wait()

    @pl.loop(0, rows // ROWS)
    def _(i):
        here = at(i, ROWS)
        v = tok[here, :].astype(F32)
        mean = jnp.mean(v, axis=-1, keepdims=True)
        centre = v - mean
        r = lax.rsqrt(jnp.mean(centre * centre, axis=-1, keepdims=True) + epsilon)
        normed = (centre * r * ln1_gain + ln1_bias).astype(BF)
        n1[here, :] = normed
        n1_t[:, here] = normed.T
        stats[0, here, :] = jnp.broadcast_to(mean, (ROWS, BLOCK))
        stats[1, here, :] = jnp.broadcast_to(r, (ROWS, BLOCK))

    first_head = lax.broadcasted_iota(jnp.int32, (BLOCK, heads_w), 1) < HD

    def two_heads(block):
        zero = jnp.zeros_like(block)
        return jnp.concatenate(
            [jnp.where(first_head, block, zero), jnp.where(first_head, zero, block)], axis=0
        )

    def pick_heads(both):
        own = jnp.concatenate([both[:HD, :BLOCK], both[HD:, BLOCK:]], axis=0)
        return own.T

    def project_heads(s):
        @pl.loop(0, rows // ROWS)
        def _(i):
            here = at(i, ROWS)
            got = mm(n1[here, :], wq[s])
            qs[s, here, :] = got[:, :heads_w].astype(BF) * jnp.asarray(HD**-0.5, BF)
            k = got[:, heads_w : 2 * heads_w].astype(BF)
            v = got[:, 2 * heads_w :].astype(BF)
            there = at(i, ROWS, BLOCK)
            ks[s, there, :] = k
            vs[s, there, :] = v
            ks_t[s, :, there] = k.T
            vs_t[s, :, there] = v.T

    def attend_slot(s):
        @pl.loop(0, blocks)
        def _(i):
            here = at(i, BLOCK)
            seen = pl.ds(pl.multiple_of(i * BLOCK, BLOCK), 2 * BLOCK)
            one = bias[i]
            scores = mm_nt(ks[s, seen, :], two_heads(qs[s, here, :]))
            scores = scores + jnp.concatenate([one, one], axis=1)
            peak = jnp.max(scores, axis=0, keepdims=True)
            expo = jnp.exp(scores - peak)
            total = jnp.sum(expo, axis=0, keepdims=True)
            low = (expo * (1.0 / total)).astype(BF)
            probs[s, i] = low
            mixed[here, s * heads_w : (s + 1) * heads_w] = pick_heads(
                mm(vs_t[s, :, seen], low)
            ).astype(BF)

    load_wq.wait()
    project_heads(0)
    attend_slot(0)
    gather_first("wq")
    gather_send("wp")
    gather_send("wu")
    gather_wait("wq", 1)
    project_heads(1)
    attend_slot(1)
    gather_second("wq")
    for s in range(2, n_t):
        if s == 3:
            gather_first("wp")
            gather_first("wu")
            gather_send("wd")
        gather_wait("wq", s)
        project_heads(s)
        attend_slot(s)
    gather_second("wp")
    gather_second("wu")

    load_wp.wait()
    load_dy.wait()
    for s in range(1, n_t):
        gather_wait("wp", s)

    @pl.loop(0, rows // ROWS)
    def _(i):
        here = at(i, ROWS)
        v = tok[here, :].astype(F32) + proj_bias
        v = v + mm(mixed[here, :], wp[...].reshape(n_t * heads_w, width))
        hidden[here, :] = v
        mean = jnp.mean(v, axis=-1, keepdims=True)
        centre = v - mean
        r = lax.rsqrt(jnp.mean(centre * centre, axis=-1, keepdims=True) + epsilon)
        normed = (centre * r * ln2_gain + ln2_bias).astype(BF)
        n2[here, :] = normed
        n2_t[:, here] = normed.T
        stats[2, here, :] = jnp.broadcast_to(mean, (ROWS, BLOCK))
        stats[3, here, :] = jnp.broadcast_to(r, (ROWS, BLOCK))
        dy_t[:, here] = dy[here, :].T

    def mlp_slot(s):
        @pl.loop(0, rows // ROWS)
        def _(i):
            here = at(i, ROWS)
            u = mm(n2[here, :], wu[s]) + bu[s, 0:1, :]
            dact = mm_nt(dy[here, :], wd[s])
            cdf, bell = normal_parts(u)
            active = (u * cdf).astype(BF)
            du = (dact * (cdf + bell)).astype(BF)
            act[here, :] = active
            dup[here, :] = du
            bup_acc[s] += by_eight(du.astype(F32))
            up_part = mm(active, wd[s])
            back_part = mm_nt(du, wu[s])
            if s == 0:
                out_acc[here, :] = up_part
                dn2_acc[here, :] = back_part
            else:
                out_acc[here, :] += up_part
                dn2_acc[here, :] += back_part

        tile = 2 * n_x * m_own.shape[3]

        @pl.loop(0, width // tile)
        def _(j):
            here = at(j, tile)
            split = (2, n_x, m_own.shape[3], hidden_w)
            m_own[s, pl.ds(2 * j, 2), :, :, 0:hidden_w] = (
                mm(n2_t[here, :], dup[...]).astype(BF).reshape(split)
            )
            m_own[s, pl.ds(2 * j, 2), :, :, hidden_w:] = (
                mm(dy_t[here, :], act[...]).astype(BF).reshape(split)
            )

    def rs_core_send(tag, own, got, k):
        copies.start((tag, "c", k), own.at[CORES * k + 1], got.at[k], core)

    def rs_x_send(tag, own, got, after, k):
        copies.arrived((tag, "c", k), got.at[k], core)

        @pl.loop(0, n_z)
        def _(a):
            own[CORES * k, a] = own[CORES * k, a] + got[k, a]

        for j in range(1, n_x):
            which = lax.rem(x + j, n_x)
            copies.start(
                (tag, "x", k, j), own.at[CORES * k, :, which], after.at[k, j - 1], x_peer(j)
            )

    def rs_x_sum(tag, own, after, k):
        for j in range(1, n_x):
            copies.arrived((tag, "x", k, j), after.at[k, j - 1], core)

        @pl.loop(0, n_z)
        def _(a):
            total = own[CORES * k, a, x].astype(F32)
            for j in range(1, n_x):
                total = total + after[k, j - 1, a].astype(F32)
            after[k, 0, a] = total.astype(BF)

    def rs_y_send(tag, after, got, k):
        copies.start((tag, "y", k), after.at[k, 0], got.at[k - 1], t_peer(k, 0))

    def rs_z_send(tag, after, got, last):
        for k in range(1, n_y):
            copies.arrived((tag, "y", k), got.at[k - 1], core)

        @pl.loop(0, n_z)
        def _(a):
            total = after[0, 0, a].astype(F32)
            for k in range(1, n_y):
                total = total + got[k - 1, a].astype(F32)
            after[0, 0, a] = total.astype(BF)

        for k in range(1, n_z):
            copies.start(
                (tag, "z", k), after.at[0, 0, lax.rem(z + k, n_z)], last.at[k - 1], z_peer(k)
            )

    def rs_finish(tag, after, last, result):
        for k in range(1, n_z):
            copies.arrived((tag, "z", k), last.at[k - 1], core)
        total = after[0, 0, z].astype(F32)
        for k in range(1, n_z):
            total = total + last[k - 1].astype(F32)
        result[...] = total

    load_wu.wait()
    load_wd.wait()
    for s in range(1, n_t):
        copies.arrived(("bu", s), bu.at[s], core)
    gather_first("wd")
    mlp_slot(0)
    gather_second("wd")
    for s in range(1, n_t):
        gather_wait("wu", s)
        gather_wait("wd", s)
        mlp_slot(s)
        if s % CORES == 1:
            rs_core_send("m", m_own, m_core, s // CORES)
        elif s >= 2:
            rs_x_send("m", m_own, m_core, m_x, s // CORES - 1)
    rs_x_send("m", m_own, m_core, m_x, n_y - 1)

    @pl.loop(0, rows // ROWS)
    def _(i):
        here = at(i, ROWS)
        value = hidden[here, :]
        out_b[here, :] = (value + out_acc[here, :] + down_bias).astype(BF)
        mean = stats[2, here, 0:1]
        r = stats[3, here, 0:1]
        xhat = (value - mean) * r
        dn = dn2_acc[here, :]
        g = dy[here, :].astype(F32)
        scaled = dn * ln2_gain
        first = jnp.mean(scaled, axis=-1, keepdims=True)
        second = jnp.mean(scaled * xhat, axis=-1, keepdims=True)
        dh = g + r * (scaled - first - xhat * second)
        hidden[here, :] = dh
        low = dh.astype(BF)
        dy_t[:, here] = low.T
        dmixed[here, :] = mm_nt(low, wp[...].reshape(n_t * heads_w, width)).astype(BF)
        vec_acc[2] += by_eight(dh)
        vec_acc[3] += by_eight(dn * xhat)
        vec_acc[4] += by_eight(dn)
        vec_acc[5] += by_eight(g)

    store_out = local(out_b, out_h, 6)

    qkv_w = 3 * heads_w
    tile = 2 * n_x * q_own.shape[3]

    @pl.loop(0, width // tile)
    def _(j):
        got = mm(dy_t[at(j, tile), :], mixed[...]).astype(BF)
        for s in range(n_t):
            q_own[s, pl.ds(2 * j, 2), :, :, qkv_w:] = got[
                :, s * heads_w : (s + 1) * heads_w
            ].reshape(2, n_x, q_own.shape[3], heads_w)

    def attend_back_slot(s):
        carry[...] = jnp.zeros_like(carry)

        @pl.loop(0, blocks)
        def _(i):
            here = at(i, BLOCK)
            seen = pl.ds(pl.multiple_of(i * BLOCK, BLOCK), 2 * BLOCK)
            grad = two_heads(dmixed[here, s * heads_w : (s + 1) * heads_w])
            low = probs[s, i]
            p = low.astype(F32)
            weighed = p * mm_nt(vs[s, seen, :], grad)
            ds = (weighed - p * jnp.sum(weighed, axis=0, keepdims=True)).astype(BF)
            dv = mm(low, grad)
            dk = mm(ds, two_heads(qs[s, here, :]))
            dq = pick_heads(mm(ks_t[s, :, seen], ds)) * (HD**-0.5)
            dtri[s, at(i, BLOCK, BLOCK), 0:heads_w] = dq.astype(BF)
            dtri[s, here, heads_w : 2 * heads_w] = (carry[0] + dk[:BLOCK]).astype(BF)
            dtri[s, here, 2 * heads_w :] = (carry[1] + dv[:BLOCK]).astype(BF)
            carry[0] = dk[BLOCK:]
            carry[1] = dv[BLOCK:]

        dtri[s, rows:, heads_w : 2 * heads_w] = carry[0].astype(BF)
        dtri[s, rows:, 2 * heads_w :] = carry[1].astype(BF)

        @pl.loop(0, width // tile)
        def _(j):
            q_own[s, pl.ds(2 * j, 2), :, :, 0:qkv_w] = (
                mm(n1_t[at(j, tile), :], dtri[s, BLOCK:, :])
                .astype(BF)
                .reshape(2, n_x, q_own.shape[3], qkv_w)
            )

    for k in reversed(range(n_y)):
        attend_back_slot(CORES * k + 1)
        rs_core_send("q", q_own, q_core, k)
        rs_x_sum("m", m_own, m_x, k)
        if k > 0:
            rs_y_send("m", m_x, m_y, k)
        if k < n_y - 1:
            rs_x_sum("q", q_own, q_x, k + 1)
            rs_y_send("q", q_x, q_y, k + 1)
        attend_back_slot(CORES * k)
        rs_x_send("q", q_own, q_core, q_x, k)
    rs_z_send("m", m_x, m_y, m_z)

    @pl.loop(0, rows // ROWS)
    def _(i):
        here = at(i, ROWS)
        there = at(i, ROWS, BLOCK)
        dn = mm_nt(dtri[0, there, :], wq[0])
        for s in range(1, n_t):
            dn = dn + mm_nt(dtri[s, there, :], wq[s])
        mean = stats[0, here, 0:1]
        r = stats[1, here, 0:1]
        xhat = (tok[here, :].astype(F32) - mean) * r
        scaled = dn * ln1_gain
        first = jnp.mean(scaled, axis=-1, keepdims=True)
        second = jnp.mean(scaled * xhat, axis=-1, keepdims=True)
        gtok_b[here, :] = (hidden[here, :] + r * (scaled - first - xhat * second)).astype(BF)
        vec_acc[0] += by_eight(dn * xhat)
        vec_acc[1] += by_eight(dn)

    store_gtok = local(gtok_b, gtok_h, 7)

    for s in range(n_t):
        lines = [jnp.sum(vec_acc[k], axis=0, keepdims=True) for k in range(6)]
        lines.append(jnp.sum(bup_acc[s], axis=0, keepdims=True))
        lines.append(jnp.zeros((1, width), F32))
        vec_mine[s] = jnp.concatenate(lines, axis=0)
    for s in range(1, n_t):
        copies.start(
            ("vt", s), vec_mine.at[s], vec_t.at[s - 1], t_peer(s // CORES, s % CORES)
        )
    rs_x_sum("q", q_own, q_x, 0)
    rs_z_send("q", q_x, q_y, q_z)
    total = vec_mine[0]
    for s in range(1, n_t):
        copies.arrived(("vt", s), vec_t.at[s - 1], core)
        total = total + vec_t[s - 1]
    vec_sum[...] = total
    for k in range(1, n_dp):
        copies.start(("vd", k), vec_sum, vec_dp.at[k - 1], (lax.rem(d + k, n_dp), t))
    rs_finish("m", m_x, m_z, gm_ref)
    for k in range(1, n_dp):
        copies.arrived(("vd", k), vec_dp.at[k - 1], core)
        total = total + vec_dp[k - 1]
    gv_ref[...] = total
    rs_finish("q", q_x, q_z, gq_ref)
    store_out.wait()
    store_gtok.wait()
    copies.drain()


def fused_device(
    n_t,
    n_dp,
    tokens,
    clip_ids,
    ln1_gain,
    ln1_bias,
    query_key_value_weight,
    projection_weight,
    attention_output_bias,
    ln2_gain,
    ln2_bias,
    up_weight,
    mlp_up_bias,
    down_weight,
    mlp_down_bias,
    grad_output,
):
    _, rows, width = tokens.shape
    heads_w = projection_weight.shape[0]
    hidden_w = up_weight.shape[1]
    n_y, n_x, n_z = n_t // CORES, WIDE, n_dp // WIDE
    part = width // n_dp
    blocks = rows // BLOCK
    qkv_w = 3 * heads_w
    vecs = jnp.stack(
        [ln1_gain, ln1_bias, attention_output_bias, ln2_gain, ln2_bias, mlp_down_bias]
    )

    def chunk(w):
        return [
            pltpu.VMEM((n_t, n_z, n_x, part, w), BF),
            pltpu.VMEM((n_y, n_z, n_x, part, w), BF),
            pltpu.VMEM((n_y, n_x - 1, n_z, part, w), BF),
            pltpu.VMEM((n_y - 1, n_z, part, w), BF),
            pltpu.VMEM((n_z - 1, part, w), BF),
        ]

    def half(*shape):
        return pltpu.VMEM(shape, BF)

    def single(*shape):
        return pltpu.VMEM(shape, F32)

    scratch = [
        half(rows, width),
        half(rows, width),
        half(width, rows),
        half(n_t, width, qkv_w),
        half(n_t, heads_w, width),
        half(n_t, width, hidden_w),
        half(n_t, hidden_w, width),
        single(n_t, 8, hidden_w),
        half(rows, width),
        half(width, rows),
        single(4, rows, BLOCK),
        half(n_t, rows, heads_w),
        half(n_t, rows + BLOCK, heads_w),
        half(n_t, rows + BLOCK, heads_w),
        half(n_t, heads_w, rows + BLOCK),
        half(n_t, heads_w, rows + BLOCK),
        single(blocks, 2 * BLOCK, BLOCK),
        half(n_t, blocks, 2 * BLOCK, 2 * BLOCK),
        half(rows, n_t * heads_w),
        single(rows, width),
        half(rows, width),
        half(width, rows),
        single(rows, width),
        single(rows, width),
        half(rows, hidden_w),
        half(rows, hidden_w),
        half(rows, n_t * heads_w),
        half(n_t, rows + BLOCK, qkv_w),
        single(2, BLOCK, heads_w),
        single(6, 8, width),
        single(n_t, 8, hidden_w),
        single(n_t, 8, width),
        single(n_t - 1, 8, width),
        single(8, width),
        single(n_dp - 1, 8, width),
        *chunk(2 * hidden_w),
        *chunk(qkv_w + heads_w),
        half(rows, width),
        half(rows, width),
        pltpu.SemaphoreType.DMA((8,)),
        pltpu.SemaphoreType.DMA((64,)),
        pltpu.SemaphoreType.DMA((64,)),
    ]
    anywhere = pl.BlockSpec(memory_space=pl.ANY)
    near = pl.BlockSpec(memory_space=pltpu.VMEM)
    out, gtok, gm, gq, gv = pl.pallas_call(
        functools.partial(layer_kernel, (n_t, n_dp, rows, width, heads_w, hidden_w)),
        out_shape=(
            jax.ShapeDtypeStruct((rows, width), BF),
            jax.ShapeDtypeStruct((rows, width), BF),
            jax.ShapeDtypeStruct((part, 2 * hidden_w), F32),
            jax.ShapeDtypeStruct((part, qkv_w + heads_w), F32),
            jax.ShapeDtypeStruct((8, width), F32),
        ),
        in_specs=[anywhere, anywhere, near, near, near] + [anywhere] * 4,
        out_specs=(anywhere, anywhere, near, near, near),
        scratch_shapes=scratch,
        compiler_params=pltpu.CompilerParams(
            collective_id=0, has_side_effects=True, vmem_limit_bytes=63 << 20
        ),
    )(
        tokens.reshape(rows, width),
        grad_output.reshape(rows, width),
        clip_ids,
        vecs,
        mlp_up_bias.reshape(1, hidden_w),
        query_key_value_weight.reshape(width, qkv_w),
        projection_weight,
        up_weight,
        down_weight,
    )
    d, t = lax.axis_index("dp"), lax.axis_index("tensor")
    share = width // (n_dp * n_t)
    vectors = lax.dynamic_slice(gv, (0, (d * n_t + t) * share), (6, share))
    g_up_bias = lax.dynamic_slice(gv, (6, d * (hidden_w // n_dp)), (1, hidden_w // n_dp))
    return (
        out[None],
        gtok[None],
        vectors[0],
        vectors[1],
        gq[:, :qkv_w].reshape(part, 3, heads_w),
        gq[:, qkv_w:].T,
        vectors[2],
        vectors[3],
        vectors[4],
        gm[:, :hidden_w],
        g_up_bias,
        gm[:, hidden_w:].T,
        vectors[5],
    )


def fits(mesh, shapes):
    n_t, n_dp = mesh.shape["tensor"], mesh.shape["dp"]
    seqs, length, width = shapes[0]
    features = shapes[4][2] // n_t
    hidden_w = shapes[9][1] // n_t
    return (
        seqs == n_t * n_dp
        and length % ROWS == 0
        and features == 2 * HD == BLOCK
        and hidden_w == width
        and n_t % CORES == 0
        and n_t // CORES > 1
        and n_dp % (2 * WIDE) == 0
        and (width // n_dp) % 16 == 0
    )


def solution(mesh):
    in_specs = (
        P(("dp", "tensor"), None, None),
        P("dp", None),
        P(),
        P(),
        P(None, None, "tensor"),
        P("tensor", None),
        P(),
        P(),
        P(),
        P(None, "tensor"),
        P("tensor"),
        P("tensor", None),
        P(),
        P(("dp", "tensor"), None, None),
    )
    out_specs = (
        P(("dp", "tensor"), None, None),
        P(("dp", "tensor"), None, None),
        P(("dp", "tensor")),
        P(("dp", "tensor")),
        P("dp", None, "tensor"),
        P("tensor", "dp"),
        P(("dp", "tensor")),
        P(("dp", "tensor")),
        P(("dp", "tensor")),
        P("dp", "tensor"),
        P("tensor", "dp"),
        P("tensor", "dp"),
        P(("dp", "tensor")),
    )

    def run(*arrays):
        body = on_device
        if fits(mesh, [a.shape for a in arrays]):
            body = functools.partial(fused_device, mesh.shape["tensor"], mesh.shape["dp"])
        return jax.shard_map(
            body, mesh=mesh, in_specs=in_specs, out_specs=out_specs, check_vma=False
        )(*arrays)

    return run
```

```python
import functools
import math

import jax
import jax.numpy as jnp
from jax import lax
from jax.experimental import pallas as pl
from jax.experimental.pallas import tpu as pltpu
from jax.sharding import PartitionSpec as P

HD = 64
CORES = 2
WIDE = 2
PAIR = 2
BF = jnp.bfloat16
F32 = jnp.float32
MESH = pl.DeviceIdType.MESH


epsilon = 1e-05


def layer_norm(values, gain, shift):
    centre = values - jnp.mean(values, axis=-1, keepdims=True)
    spread = jnp.mean(centre * centre, axis=-1, keepdims=True)
    return centre * lax.rsqrt(spread + epsilon) * gain + shift


def gelu_exact(values):
    return jax.nn.gelu(values, approximate=False)


def visible(clip_row, start, count):
    length = clip_row.shape[0]
    query_pos = start + jnp.arange(count)
    key_pos = jnp.arange(length)
    query_clip = clip_row[start : start + count]
    return (key_pos[None, :] <= query_pos[:, None]) & (query_clip[:, None] == clip_row[None, :])


def block_scores(query, keys, clip_row, start, block):
    scale = query.shape[-1] ** (-0.5)
    allowed = visible(clip_row, start, block)
    scores = (
        jnp.einsum(
            "qhd,khd->hqk", query[start : start + block], keys, preferred_element_type=jnp.float32
        )
        * scale
    )
    return (jnp.where(allowed[None], scores, -1e30), allowed)


def attend_sequence(pieces):
    query, keys, vals, clip_row = pieces
    length = query.shape[0]
    block = min(512, length)
    outs = []
    sums = []
    for start in range(0, length, block):
        scores, allowed = block_scores(query, keys, clip_row, start, block)
        peak = jnp.max(scores, axis=-1, keepdims=True)
        expo = jnp.exp(scores - peak)
        total = jnp.sum(expo, axis=-1, keepdims=True)
        probs = (expo / total).astype(jnp.bfloat16)
        outs.append(jnp.einsum("hqk,khd->qhd", probs, vals, preferred_element_type=jnp.float32))
        sums.append((peak + jnp.log(total))[..., 0])
    return (jnp.concatenate(outs, 0), jnp.concatenate(sums, 1))


def attend_back(pieces):
    query, keys, vals, clip_row, lse, grad_mixed = pieces
    length = query.shape[0]
    block = min(512, length)
    scale = query.shape[-1] ** (-0.5)
    grad_keys = jnp.zeros(keys.shape, jnp.float32)
    grad_vals = jnp.zeros(vals.shape, jnp.float32)
    query_parts = []
    for start in range(0, length, block):
        scores, allowed = block_scores(query, keys, clip_row, start, block)
        probs_f = jnp.where(
            allowed[None], jnp.exp(scores - lse[:, start : start + block, None]), 0.0
        )
        probs = probs_f.astype(jnp.bfloat16)
        grad_block = grad_mixed[start : start + block]
        dprobs = jnp.einsum("qhd,khd->hqk", grad_block, vals, preferred_element_type=jnp.float32)
        grad_vals = grad_vals + jnp.einsum(
            "hqk,qhd->khd", probs, grad_block, preferred_element_type=jnp.float32
        )
        inner = jnp.sum(probs_f * dprobs, axis=-1, keepdims=True)
        dscores = (probs_f * (dprobs - inner)).astype(jnp.bfloat16)
        query_parts.append(
            jnp.einsum("hqk,khd->qhd", dscores, keys, preferred_element_type=jnp.float32) * scale
        )
        grad_keys = (
            grad_keys
            + jnp.einsum(
                "hqk,qhd->khd",
                dscores,
                query[start : start + block],
                preferred_element_type=jnp.float32,
            )
            * scale
        )
    return (jnp.concatenate(query_parts, 0), grad_keys, grad_vals)


def on_device(
    tokens,
    clip_ids,
    ln1_gain,
    ln1_bias,
    query_key_value_weight,
    projection_weight,
    attention_output_bias,
    ln2_gain,
    ln2_bias,
    up_weight,
    mlp_up_bias,
    down_weight,
    mlp_down_bias,
    grad_output,
):
    head_size = HD
    local_width = query_key_value_weight.shape[2]
    local_heads = local_width // head_size
    tok_f = tokens.astype(jnp.float32)
    first_normalized = layer_norm(tok_f, ln1_gain, ln1_bias).astype(jnp.bfloat16)
    first_normalized_every = lax.all_gather(first_normalized, "tensor", axis=0, tiled=True)
    seqs = first_normalized_every.shape[0]
    length = first_normalized_every.shape[1]
    query_key_value_rows = jnp.einsum(
        "tre,eub->trub",
        first_normalized_every,
        query_key_value_weight,
        preferred_element_type=jnp.float32,
    ).astype(jnp.bfloat16)
    query_key_value_rows = query_key_value_rows.reshape(seqs, length, 3, local_heads, head_size)
    query = query_key_value_rows[:, :, 0]
    keys = query_key_value_rows[:, :, 1]
    vals = query_key_value_rows[:, :, 2]
    mixed_heads_output, lse = lax.map(attend_sequence, (query, keys, vals, clip_ids))
    mixed_heads_lowered = mixed_heads_output.astype(jnp.bfloat16).reshape(seqs, length, local_width)
    attention_piece = jnp.einsum(
        "bne,eo->bno", mixed_heads_lowered, projection_weight, preferred_element_type=jnp.float32
    )
    attn_rows = lax.psum_scatter(
        attention_piece.astype(jnp.bfloat16), "tensor", scatter_dimension=0, tiled=True
    ).astype(jnp.float32)
    hidden_activation = tok_f + attn_rows + attention_output_bias
    second_normalized = layer_norm(hidden_activation, ln2_gain, ln2_bias).astype(jnp.bfloat16)
    second_normalized_every = lax.all_gather(second_normalized, "tensor", axis=0, tiled=True)
    upper_half_rows = (
        jnp.einsum(
            "wih,hm->wim", second_normalized_every, up_weight, preferred_element_type=jnp.float32
        )
        + mlp_up_bias
    )
    active_rows_now = gelu_exact(upper_half_rows).astype(jnp.bfloat16)
    perceptron_piece = jnp.einsum(
        "bne,eo->bno", active_rows_now, down_weight, preferred_element_type=jnp.float32
    )
    mlp_rows = lax.psum_scatter(
        perceptron_piece.astype(jnp.bfloat16), "tensor", scatter_dimension=0, tiled=True
    ).astype(jnp.float32)
    output = (hidden_activation + mlp_rows + mlp_down_bias).astype(jnp.bfloat16)
    gradient_every_row = lax.all_gather(grad_output, "tensor", axis=0, tiled=True)
    down_weight_gradient = jnp.einsum(
        "egz,egb->zb", active_rows_now, gradient_every_row, preferred_element_type=jnp.float32
    )
    gradient_active_rows = jnp.einsum(
        "etk,ok->eto", gradient_every_row, down_weight, preferred_element_type=jnp.float32
    )
    gradient_upper_half = jax.vjp(gelu_exact, upper_half_rows)[1](gradient_active_rows)[0].astype(
        jnp.bfloat16
    )
    g_up_bias = jnp.sum(gradient_upper_half, axis=(0, 1), dtype=jnp.float32)
    up_weight_gradient = jnp.einsum(
        "kjy,kjt->yt",
        second_normalized_every,
        gradient_upper_half,
        preferred_element_type=jnp.float32,
    )
    grad_normed2_part = jnp.einsum(
        "hwm,bm->hwb", gradient_upper_half, up_weight, preferred_element_type=jnp.float32
    )
    grad_normed2 = lax.psum_scatter(
        grad_normed2_part.astype(jnp.bfloat16), "tensor", scatter_dimension=0, tiled=True
    ).astype(jnp.float32)
    grad_hidden_ln, g_ln2_gain, g_ln2_bias = jax.vjp(
        layer_norm, hidden_activation, ln2_gain, ln2_bias
    )[1](grad_normed2)
    grad_f = grad_output.astype(jnp.float32)
    grad_hidden = grad_f + grad_hidden_ln
    g_down_bias = jnp.sum(grad_f, axis=(0, 1))
    g_proj_bias = jnp.sum(grad_hidden, axis=(0, 1))
    branch_low = grad_hidden.astype(jnp.bfloat16)
    branch_every_row = lax.all_gather(branch_low, "tensor", axis=0, tiled=True)
    projection_weight_gradient = jnp.einsum(
        "egz,egb->zb", mixed_heads_lowered, branch_every_row, preferred_element_type=jnp.float32
    )
    grad_mixed = jnp.einsum(
        "etk,ok->eto", branch_every_row, projection_weight, preferred_element_type=jnp.float32
    ).astype(jnp.bfloat16)
    grad_mixed = grad_mixed.reshape(seqs, length, local_heads, head_size)
    grad_query, grad_keys, grad_vals = lax.map(
        attend_back, (query, keys, vals, clip_ids, lse, grad_mixed)
    )
    gradient_query_key_value = (
        jnp.stack((grad_query, grad_keys, grad_vals), axis=2)
        .astype(jnp.bfloat16)
        .reshape(seqs, length, 3, local_width)
    )
    query_key_value_gradient = jnp.einsum(
        "zny,znqj->yqj",
        first_normalized_every,
        gradient_query_key_value,
        preferred_element_type=jnp.float32,
    )
    grad_normed_part = jnp.einsum(
        "kegu,hgu->keh",
        gradient_query_key_value,
        query_key_value_weight,
        preferred_element_type=jnp.float32,
    )
    grad_normed = lax.psum_scatter(
        grad_normed_part.astype(jnp.bfloat16), "tensor", scatter_dimension=0, tiled=True
    ).astype(jnp.float32)
    grad_tok_ln, g_ln1_gain, g_ln1_bias = jax.vjp(layer_norm, tok_f, ln1_gain, ln1_bias)[1](
        grad_normed
    )
    grad_tokens = (grad_hidden + grad_tok_ln).astype(jnp.bfloat16)
    g_qkv_s, g_proj_s, g_up_s, g_up_bias_s, g_down_s = (
        lax.psum_scatter(
            query_key_value_gradient.astype(jnp.bfloat16), "dp", scatter_dimension=0, tiled=True
        ).astype(jnp.float32),
        lax.psum_scatter(
            projection_weight_gradient.astype(jnp.bfloat16), "dp", scatter_dimension=1, tiled=True
        ).astype(jnp.float32),
        lax.psum_scatter(
            up_weight_gradient.astype(jnp.bfloat16), "dp", scatter_dimension=0, tiled=True
        ).astype(jnp.float32),
        lax.psum_scatter(
            g_up_bias[None].astype(jnp.bfloat16), "dp", scatter_dimension=1, tiled=True
        ).astype(jnp.float32),
        lax.psum_scatter(
            down_weight_gradient.astype(jnp.bfloat16), "dp", scatter_dimension=1, tiled=True
        ).astype(jnp.float32),
    )
    v_ln1_gain, v_ln1_bias, v_proj_bias, v_ln2_gain, v_ln2_bias, v_down_bias = (
        lax.psum_scatter(g_ln1_gain, ("dp", "tensor"), scatter_dimension=0, tiled=True),
        lax.psum_scatter(g_ln1_bias, ("dp", "tensor"), scatter_dimension=0, tiled=True),
        lax.psum_scatter(g_proj_bias, ("dp", "tensor"), scatter_dimension=0, tiled=True),
        lax.psum_scatter(g_ln2_gain, ("dp", "tensor"), scatter_dimension=0, tiled=True),
        lax.psum_scatter(g_ln2_bias, ("dp", "tensor"), scatter_dimension=0, tiled=True),
        lax.psum_scatter(g_down_bias, ("dp", "tensor"), scatter_dimension=0, tiled=True),
    )
    return (
        output,
        grad_tokens,
        v_ln1_gain,
        v_ln1_bias,
        g_qkv_s,
        g_proj_s,
        v_proj_bias,
        v_ln2_gain,
        v_ln2_bias,
        g_up_s,
        g_up_bias_s,
        g_down_s,
        v_down_bias,
    )


BLOCK = 128
ROWS = 256
WIDE_ROWS = 512

ORDER = {"u": "xylh", "d": "lxyh", "p": "xylh", "qk": "xylh", "v": "lyxh"}
SCHEDULE = {
    "start": ("wq", "wp",),
    "heads0": ("wq",),
    "attend0": ("wp", "wd", "wq", "wu",),
    "attend1": ("wq", "wp",),
    "heads2": ("wd",),
    "attend2": ("wp",),
    "hidden": ("wu",),
    "mlp1": ("wd",),
    "rows0.0": ("wu", "d0",),
    "rows0.1": ("u0", "wd",),
    "mlp0": ("wu", "d0", "u0",),
    "rows2.1": ("d1", "d0", "u0", "u1",),
    "mlp2": ("u1", "d1",),
    "proj": ("p1",),
    "back3": ("p0", "p1", "d0",),
    "qkv3": ("qk1", "p0", "u1",),
    "back2": ("d1",),
    "qkv2": ("qk1",),
    "back1": ("v1", "p1", "p0",),
    "qkv1": ("qk0", "v1", "v0", "d1",),
    "back0": ("p", "qk1", "u", "v1",),
    "qkv0": ("qk0", "v0", "p", "d",),
    "norm1.1": ("vec", "qk0", "qk", "u", "v0", "v", "v", "p",),
    "end": ("vec", "qk", "v", "u", "d", "vec", "qk",),
}


def mm(left, right):
    return lax.dot_general(left, right, (((1,), (0,)), ((), ())), preferred_element_type=F32)


def mm_nt(left, right):
    return lax.dot_general(left, right, (((1,), (1,)), ((), ())), preferred_element_type=F32)


def mm_tn(left, right):
    return lax.dot_general(left, right, (((0,), (0,)), ((), ())), preferred_element_type=F32)


def normal_parts(u):
    cdf = 0.5 + 0.5 * lax.erf(u * math.sqrt(0.5))
    bell = jnp.exp2(u * u * (-0.5 * math.log2(math.e)))
    return cdf, u * bell * (1.0 / math.sqrt(2.0 * math.pi))


def by_eight(values):
    return jnp.sum(values.reshape(-1, 8, values.shape[-1]), axis=0)


class Copies:
    def __init__(self, send, recv):
        self.send, self.recv, self.made, self.started = send, recv, {}, []

    def describe(self, name, src, dst, device):
        at = self.made.setdefault(name, len(self.made))
        return pltpu.make_async_remote_copy(
            src_ref=src,
            dst_ref=dst,
            send_sem=self.send.at[at],
            recv_sem=self.recv.at[at],
            device_id=device,
            device_id_type=MESH,
        )

    def start(self, name, src, dst, device):
        copy = self.describe(name, src, dst, device)
        copy.start()
        self.started.append(copy)

    def arrived(self, name, dst, device):
        self.describe(name, dst, dst, device).wait_recv()

    def drain(self):
        for copy in self.started:
            copy.wait_send()


def layer_kernel(
    sizes,
    tok_h,
    dy_h,
    clip_ref,
    ln1_gain_ref,
    ln1_bias_ref,
    proj_bias_ref,
    ln2_gain_ref,
    ln2_bias_ref,
    down_bias_ref,
    bu_ref,
    wq_h,
    wp_h,
    wu_h,
    wd_h,
    out_h,
    gtok_h,
    gq_ref,
    gp_ref,
    gu_ref,
    gd_ref,
    gv_ref,
    tok,
    dy,
    wq,
    wp,
    wu,
    wd,
    bu,
    n1,
    stats,
    qs,
    ks,
    vs,
    ks_t,
    vs_t,
    bias,
    probs,
    mixed,
    hidden,
    n2,
    out_acc,
    dn2_acc,
    act,
    dup,
    branch,
    dmixed,
    dtri,
    vec_acc,
    bup_acc,
    vec_mine,
    vec_t,
    vec_sum,
    vec_dp,
    u_bufs,
    d_bufs,
    p_bufs,
    qk_bufs,
    v_bufs,
    out_b,
    gtok_b,
    local_sem,
    send_sem,
    recv_sem,
):
    n_t, n_dp, rows, width, heads_w, hidden_w = sizes
    n_y, n_x, n_l, n_h = n_t // CORES, WIDE, PAIR, n_dp // (WIDE * PAIR)
    blocks = rows // BLOCK
    part = width // n_dp
    qkv_w = 3 * heads_w
    d, t = lax.axis_index("dp"), lax.axis_index("tensor")
    y, c = t // CORES, lax.rem(t, CORES)
    z, x = d // WIDE, lax.rem(d, WIDE)
    z_far, z_near = z // n_l, lax.rem(z, n_l)

    def t_peer(dy_, dc_):
        return (d, lax.rem(y + dy_, n_y) * CORES + lax.rem(c + dc_, CORES))

    def x_peer(k):
        return (z * WIDE + lax.rem(x + k, n_x), t)

    def l_peer(k):
        return ((z_far * n_l + lax.rem(z_near + k, n_l)) * WIDE + x, t)

    def h_peer(k):
        return ((lax.rem(z_far + k, n_h) * n_l + z_near) * WIDE + x, t)

    peers = [t_peer(s // CORES, s % CORES) for s in range(1, n_t)]
    peers += [(lax.rem(d + k, n_dp), t) for k in range(1, n_dp)]
    core = t_peer(0, 1)

    barrier = pltpu.get_barrier_semaphore()
    for peer in peers:
        pl.semaphore_signal(barrier, inc=1, device_id=peer, device_id_type=MESH)

    def local(src, dst, at):
        copy = pltpu.make_async_copy(src, dst, local_sem.at[at])
        copy.start()
        return copy

    load_tok = local(tok_h, tok, 0)
    load_wq = local(wq_h, wq.at[0], 1)
    load_wp = local(wp_h, wp.at[0], 2)
    load_dy = local(dy_h, dy, 3)
    load_wu = local(wu_h, wu.at[0], 4)
    load_wd = local(wd_h, wd.at[0], 5)
    bu[0] = jnp.broadcast_to(bu_ref[...], bu.shape[1:])

    ln1_gain, ln1_bias = ln1_gain_ref[...], ln1_bias_ref[...]
    proj_bias = proj_bias_ref[...]
    ln2_gain, ln2_bias = ln2_gain_ref[...], ln2_bias_ref[...]
    down_bias = down_bias_ref[...]
    vec_acc[...] = jnp.zeros_like(vec_acc)
    bup_acc[...] = jnp.zeros_like(bup_acc)

    clip = clip_ref[pl.ds(t, 1), :].astype(F32)
    key_at = lax.broadcasted_iota(jnp.int32, (BLOCK, BLOCK), 0)
    query_at = lax.broadcasted_iota(jnp.int32, (BLOCK, BLOCK), 1)
    before = jnp.full((BLOCK, BLOCK), -1.0, F32)
    for i in range(blocks):
        row = clip[:, i * BLOCK : (i + 1) * BLOCK]
        ids = jnp.broadcast_to(row, (BLOCK, BLOCK))
        down = ids.T
        bias[i, 0:BLOCK, :] = jnp.where(before == ids, 0.0, -1e30)
        bias[i, BLOCK:, :] = jnp.where((down == ids) & (key_at <= query_at), 0.0, -1e30)
        before = down

    for s in range(n_t):
        ks[s, 0:BLOCK, :] = jnp.zeros((BLOCK, heads_w), BF)
        vs[s, 0:BLOCK, :] = jnp.zeros((BLOCK, heads_w), BF)
        ks_t[s, :, 0:BLOCK] = jnp.zeros((heads_w, BLOCK), BF)
        vs_t[s, :, 0:BLOCK] = jnp.zeros((heads_w, BLOCK), BF)

    def at(i, size, offset=0):
        return pl.ds(pl.multiple_of(i * size + offset, math.gcd(size, offset) if offset else size), size)

    load_tok.wait()

    @pl.loop(0, rows // ROWS)
    def _(i):
        here = at(i, ROWS)
        v = tok[here, :].astype(F32)
        mean = jnp.mean(v, axis=-1, keepdims=True)
        centre = v - mean
        r = lax.rsqrt(jnp.mean(centre * centre, axis=-1, keepdims=True) + epsilon)
        normed = (centre * r * ln1_gain + ln1_bias).astype(BF)
        n1[here, :] = normed
        stats[0, here, :] = jnp.broadcast_to(mean, (ROWS, BLOCK))
        stats[1, here, :] = jnp.broadcast_to(r, (ROWS, BLOCK))

    pl.semaphore_wait(barrier, len(peers))
    copies = Copies(send_sem, recv_sem)

    full = {"wq": (wq_h, wq), "wp": (wp_h, wp), "wu": (wu_h, wu), "wd": (wd_h, wd)}

    def rows_of(ref, which, parts):
        part = ref.shape[-2] // parts
        here = pl.ds(pl.multiple_of(which * part, part), part)
        return ref.at[:, here] if len(ref.shape) == 3 else ref.at[here]

    def gather(name):
        src, dst = full[name]
        quarters, mine = n_x * n_l, x * n_l + z_near
        across, along = lax.rem(x + 1, n_x) * n_l + z_near, x * n_l + lax.rem(z_near + 1, n_l)
        last = lax.rem(x + 1, n_x) * n_l + lax.rem(z_near + 1, n_l)

        def spot(k, which, halves=1, half=0):
            return rows_of(dst.at[CORES * k], which * halves + half, quarters * halves)

        def pass_on(k, n):
            which = (mine, across, along, last)[n]
            there = rows_of(dst.at[CORES * k + 1], which, quarters)
            copies.start((name, "core", k, n), spot(k, which), there, core)

        far = range(1, n_y)
        copies.start((name, "core", 0), src, dst.at[1], core)
        for k in far:
            copies.start(
                (name, "y", k), rows_of(src, mine, quarters), spot(k, mine), t_peer(n_y - k, 0)
            )
        yield
        for k in far:
            copies.arrived((name, "y", k), spot(k, mine), core)
            copies.start((name, "x", k), spot(k, mine), spot(k, mine), x_peer(1))
            copies.start((name, "l", k), spot(k, mine), spot(k, mine), l_peer(1))
            pass_on(k, 0)
        yield
        for k in far:
            copies.arrived((name, "x", k), spot(k, across), core)
            first = spot(k, across, 2, 0)
            copies.start((name, "xl", k), first, first, l_peer(1))
            copies.arrived((name, "l", k), spot(k, along), core)
            second = spot(k, along, 2, 1)
            copies.start((name, "lx", k), second, second, x_peer(1))
            pass_on(k, 1)
            pass_on(k, 2)
        yield
        for k in far:
            copies.arrived((name, "xl", k), spot(k, last, 2, 0), core)
            copies.arrived((name, "lx", k), spot(k, last, 2, 1), core)
            pass_on(k, 3)
        yield

    def whole(name, s):
        _, dst = full[name]
        quarters = n_x * n_l
        if s == 1:
            copies.arrived((name, "core", 0), dst.at[1], core)
        elif s % CORES == 1:
            here, there = lax.rem(x + 1, n_x) * n_l, lax.rem(z_near + 1, n_l)
            spots = [x * n_l + z_near, here + z_near, x * n_l + there, here + there]
            for n, which in enumerate(spots):
                got = rows_of(dst.at[s], which, quarters)
                copies.arrived((name, "core", s // CORES, n), got, core)

    position = {"x": x, "l": z_near, "h": z_far}
    extent = {"x": n_x, "l": n_l, "h": n_h}
    neighbour = {"x": x_peer, "l": l_peer, "h": h_peer}
    reduced = {}

    def take(ref, dims, axis, which):
        return ref.at[(slice(None),) * dims.index(axis) + (which,)]

    def spots_of(dims):
        spots = [()]
        for axis in dims:
            spots = [spot + (a,) for spot in spots for a in range(extent[axis])]
        return spots

    def sum_f32(values):
        return functools.reduce(lambda a, b: a + b, [v.astype(F32) for v in values])

    def send_parts(name, cur, dims, axis, recv):
        for j in range(1, extent[axis]):
            which = lax.rem(position[axis] + j, extent[axis])
            copies.start(
                (name, axis, j), take(cur, dims, axis, which), recv.at[j - 1], neighbour[axis](j)
            )

    def fold(name, cur, dims, axis, recv, keep=True):
        for j in range(1, extent[axis]):
            copies.arrived((name, axis, j), recv.at[j - 1], core)
        at_axis = dims.index(axis)
        rest = [d for d in dims if d != axis]
        total = None
        for spot in spots_of(rest):
            mine = cur[spot[:at_axis] + (position[axis],) + spot[at_axis:]]
            total = sum_f32([mine] + [recv[(j,) + spot] for j in range(extent[axis] - 1)])
            if keep:
                recv[(0,) + spot] = total.astype(BF)
        return (recv.at[0] if keep else total), rest

    def reduce_pair(tag, bufs, k):
        order = ORDER[tag]
        own, got = bufs[:2]
        copies.start((tag, "core", k), own.at[CORES * k + 1], got.at[k], core)
        yield
        copies.arrived((tag, "core", k), got.at[k], core)
        for spot in spots_of(["h", "l", "x"]):
            here = (CORES * k,) + spot
            own[here] = own[here] + got[(k,) + spot]
        cur, dims = own.at[CORES * k], ["h", "l", "x"]
        for n, axis in enumerate(order[: order.index("y")]):
            recv = bufs[2 + n].at[k]
            send_parts((tag, k), cur, dims, axis, recv)
            yield
            cur, dims = fold((tag, k), cur, dims, axis, recv)
        if k > 0:
            copies.start((tag, "y", k), cur, bufs[2 + order.index("y")].at[k - 1], t_peer(k, 0))
        reduced[tag, k] = cur, dims
        yield

    def reduce_end(tag, bufs, write):
        order = ORDER[tag]
        cur, dims = reduced[tag, 0]
        at_y = order.index("y")
        recv = bufs[2 + at_y]
        for k in range(1, n_y):
            copies.arrived((tag, "y", k), recv.at[k - 1], core)
        total = None
        for spot in spots_of(dims):
            total = sum_f32([cur[spot]] + [recv[(k,) + spot] for k in range(n_y - 1)])
            if dims:
                recv[(0,) + spot] = total.astype(BF)
        cur = recv.at[0]
        for n, axis in enumerate(order[at_y + 1 :]):
            recv = bufs[3 + at_y + n]
            send_parts(tag, cur, dims, axis, recv)
            yield
            cur, dims = fold(tag, cur, dims, axis, recv, len(dims) > 1)
            total = cur
        write(total)
        yield

    def write_up(total):
        gu_ref[...] = total

    def write_down(total):
        gd_ref[...] = total

    def write_proj(total):
        gp_ref[...] = total

    def write_query_key(total):
        gq_ref[0] = total[:, :heads_w]
        gq_ref[1] = total[:, heads_w:]

    def write_value(total):
        gq_ref[2] = total

    def vectors():
        for s in range(n_t):
            lines = [jnp.sum(vec_acc[k], axis=0, keepdims=True) for k in range(6)]
            lines.append(jnp.sum(bup_acc[s], axis=0, keepdims=True))
            lines.append(jnp.zeros((1, width), F32))
            vec_mine[s] = jnp.concatenate(lines, axis=0)
        for s in range(1, n_t):
            copies.start(("vt", s), vec_mine.at[s], vec_t.at[s - 1], t_peer(s // CORES, s % CORES))
        yield
        total = vec_mine[0]
        for s in range(1, n_t):
            copies.arrived(("vt", s), vec_t.at[s - 1], core)
            total = total + vec_t[s - 1]
        vec_sum[...] = total
        for k in range(1, n_dp):
            copies.start(("vd", k), vec_sum, vec_dp.at[k - 1], (lax.rem(d + k, n_dp), t))
        yield
        for k in range(1, n_dp):
            copies.arrived(("vd", k), vec_dp.at[k - 1], core)
            total = total + vec_dp[k - 1]
        gv_ref[...] = total
        yield

    u_own, d_own, p_own = u_bufs[0], d_bufs[0], p_bufs[0]
    qk_own, v_own = qk_bufs[0], v_bufs[0]
    sums = {
        "u": (u_bufs, write_up),
        "d": (d_bufs, write_down),
        "p": (p_bufs, write_proj),
        "qk": (qk_bufs, write_query_key),
        "v": (v_bufs, write_value),
    }
    steps = {name: gather(name) for name in full}
    for tag, (bufs, write) in sums.items():
        for k in range(n_y):
            steps[tag + str(k)] = reduce_pair(tag, bufs, k)
        steps[tag] = reduce_end(tag, bufs, write)
    steps["vec"] = vectors()

    def tick(name):
        for step in SCHEDULE.get(name, ()):
            next(steps[step])

    tick("start")
    for s in range(1, n_t):
        copies.start(
            ("bu", s),
            bu.at[0],
            bu.at[s],
            t_peer((n_y - s // CORES) % n_y, (CORES - s % CORES) % CORES),
        )

    first_head = lax.broadcasted_iota(jnp.int32, (BLOCK, heads_w), 1) < HD

    def two_heads(block):
        zero = jnp.zeros_like(block)
        return jnp.concatenate(
            [jnp.where(first_head, block, zero), jnp.where(first_head, zero, block)], axis=0
        )

    def pick_heads(both):
        own = jnp.concatenate([both[:HD, :BLOCK], both[HD:, BLOCK:]], axis=0)
        return own.T

    def qkv_weight(slots):
        return jnp.concatenate([wq[s, j] for s in slots for j in range(3)], axis=1)

    def project_heads(slots):
        @pl.loop(0, rows // WIDE_ROWS)
        def _(i):
            here = at(i, WIDE_ROWS)
            there = at(i, WIDE_ROWS, BLOCK)
            all_of = mm(n1[here, :], qkv_weight(slots)).astype(BF)
            for n, s in enumerate(slots):
                got = all_of[:, n * qkv_w : (n + 1) * qkv_w]
                qs[s, here, :] = got[:, :heads_w] * jnp.asarray(HD**-0.5, BF)
                k = got[:, heads_w : 2 * heads_w]
                v = got[:, 2 * heads_w :]
                ks[s, there, :] = k
                vs[s, there, :] = v
                ks_t[s, :, there] = k.T
                vs_t[s, :, there] = v.T

    heres = [pl.ds(i * BLOCK, BLOCK) for i in range(blocks)]
    seens = [pl.ds(i * BLOCK, 2 * BLOCK) for i in range(blocks)]

    def attend_slot(s):
        scores = [
            mm_nt(ks[s, seen, :], two_heads(qs[s, here, :])) for here, seen in zip(heres, seens)
        ]
        lows = []
        for i in range(blocks):
            one = bias[i]
            score = scores[i] + jnp.concatenate([one, one], axis=1)
            expo = jnp.exp(score - jnp.max(score, axis=0, keepdims=True))
            total = jnp.sum(expo, axis=0, keepdims=True)
            low = (expo * (1.0 / total)).astype(BF)
            probs[s, i] = low
            lows.append(low)
        both = [mm(vs_t[s, :, seen], low) for seen, low in zip(seens, lows)]
        for i in range(blocks):
            mixed[heres[i], s * heads_w : (s + 1) * heads_w] = pick_heads(both[i]).astype(BF)

    load_wq.wait()
    whole("wq", 1)
    project_heads((0, 1))
    tick("heads0")
    attend_slot(0)
    tick("attend0")
    attend_slot(1)
    tick("attend1")
    for k in range(1, n_y):
        slots = (CORES * k, CORES * k + 1)
        whole("wq", slots[0])
        whole("wq", slots[1])
        project_heads(slots)
        tick(f"heads{slots[0]}")
        for s in slots:
            attend_slot(s)
            tick(f"attend{s}")

    load_wp.wait()
    load_dy.wait()
    for s in range(1, n_t):
        whole("wp", s)

    @pl.loop(0, rows // ROWS)
    def _(i):
        here = at(i, ROWS)
        v = tok[here, :].astype(F32) + proj_bias
        v = v + mm(mixed[here, :], wp[...].reshape(n_t * heads_w, width))
        hidden[here, :] = v
        mean = jnp.mean(v, axis=-1, keepdims=True)
        centre = v - mean
        r = lax.rsqrt(jnp.mean(centre * centre, axis=-1, keepdims=True) + epsilon)
        normed = (centre * r * ln2_gain + ln2_bias).astype(BF)
        n2[here, :] = normed
        stats[2, here, :] = jnp.broadcast_to(mean, (ROWS, BLOCK))
        stats[3, here, :] = jnp.broadcast_to(r, (ROWS, BLOCK))

    tick("hidden")

    def mlp_slot(s, new):
        for i in range(rows // WIDE_ROWS):
            here = pl.ds(i * WIDE_ROWS, WIDE_ROWS)
            u = mm(n2[here, :], wu[s]) + bu[s, 0:1, :]
            dact = mm_nt(dy[here, :], wd[s])
            cdf, bell = normal_parts(u)
            active = (u * cdf).astype(BF)
            du = (dact * (cdf + bell)).astype(BF)
            act[here, :] = active
            dup[here, :] = du
            bup_acc[s] += by_eight(du.astype(F32))
            up_part = mm(active, wd[s])
            back_part = mm_nt(du, wu[s])
            if new:
                out_acc[here, :] = up_part
                dn2_acc[here, :] = back_part
            else:
                out_acc[here, :] += up_part
                dn2_acc[here, :] += back_part
            tick(f"rows{s}.{i}")
        split = (n_h, n_l, n_x, part, hidden_w)
        u_own[s] = mm_tn(n2[...], dup[...]).astype(BF).reshape(split)
        d_own[s] = mm_tn(dy[...], act[...]).astype(BF).reshape(split)
        tick(f"mlp{s}")

    load_wu.wait()
    load_wd.wait()
    for s in range(1, n_t):
        copies.arrived(("bu", s), bu.at[s], core)
    order = [s + 1 - 2 * (s % CORES) for s in range(n_t)]
    for s in order:
        whole("wu", s)
        whole("wd", s)
        mlp_slot(s, s == order[0])

    for i in range(rows // WIDE_ROWS):
        here = pl.ds(i * WIDE_ROWS, WIDE_ROWS)
        value = hidden[here, :]
        out_b[here, :] = (value + out_acc[here, :] + down_bias).astype(BF)
        mean = stats[2, here, 0:1]
        r = stats[3, here, 0:1]
        xhat = (value - mean) * r
        dn = dn2_acc[here, :]
        g = dy[here, :].astype(F32)
        scaled = dn * ln2_gain
        first = jnp.mean(scaled, axis=-1, keepdims=True)
        second = jnp.mean(scaled * xhat, axis=-1, keepdims=True)
        dh = g + r * (scaled - first - xhat * second)
        hidden[here, :] = dh
        low = dh.astype(BF)
        branch[here, :] = low
        dmixed[here, :] = mm_nt(low, wp[...].reshape(n_t * heads_w, width)).astype(BF)
        vec_acc[2] += by_eight(dh)
        vec_acc[3] += by_eight(dn * xhat)
        vec_acc[4] += by_eight(dn)
        vec_acc[5] += by_eight(g)
        tick(f"norm2.{i}")

    store_out = local(out_b, out_h, 6)

    got = mm_tn(branch[...], mixed[...]).astype(BF)
    for s in range(n_t):
        p_own[s] = got[:, s * heads_w : (s + 1) * heads_w].reshape(n_h, n_l, n_x, part, heads_w)
    tick("proj")

    def attend_back_slot(s):
        lanes = slice(s * heads_w, (s + 1) * heads_w)
        first = s * qkv_w
        grads = [two_heads(dmixed[here, lanes]) for here in heres]
        dprobs = [mm_nt(vs[s, seen, :], grad) for seen, grad in zip(seens, grads)]
        ds = []
        for i in range(blocks):
            p = probs[s, i].astype(F32)
            weighed = p * dprobs[i]
            ds.append((weighed - p * jnp.sum(weighed, axis=0, keepdims=True)).astype(BF))
        dv = [mm(probs[s, i], grads[i]) for i in range(blocks)]
        dk = [mm(ds[i], two_heads(qs[s, heres[i], :])) for i in range(blocks)]
        dq = [pick_heads(mm(ks_t[s, :, seens[i]], ds[i])) * (HD**-0.5) for i in range(blocks)]
        for i in range(blocks):
            k_sum, v_sum = dk[i][BLOCK:], dv[i][BLOCK:]
            if i + 1 < blocks:
                k_sum, v_sum = k_sum + dk[i + 1][:BLOCK], v_sum + dv[i + 1][:BLOCK]
            dtri[heres[i], first : first + heads_w] = dq[i].astype(BF)
            dtri[heres[i], first + heads_w : first + 2 * heads_w] = k_sum.astype(BF)
            dtri[heres[i], first + 2 * heads_w : first + qkv_w] = v_sum.astype(BF)
        tick(f"back{s}")
        got = mm_tn(n1[...], dtri[:, first : first + qkv_w]).astype(BF)
        qk_own[s] = got[:, : 2 * heads_w].reshape(n_h, n_l, n_x, part, 2 * heads_w)
        v_own[s] = got[:, 2 * heads_w :].reshape(n_h, n_l, n_x, part, heads_w)
        tick(f"qkv{s}")

    for s in reversed(range(n_t)):
        attend_back_slot(s)

    for i in range(rows // WIDE_ROWS):
        here = pl.ds(i * WIDE_ROWS, WIDE_ROWS)
        dn = mm_nt(dtri[here, :], qkv_weight(range(n_t)))
        mean = stats[0, here, 0:1]
        r = stats[1, here, 0:1]
        xhat = (tok[here, :].astype(F32) - mean) * r
        scaled = dn * ln1_gain
        first = jnp.mean(scaled, axis=-1, keepdims=True)
        second = jnp.mean(scaled * xhat, axis=-1, keepdims=True)
        gtok_b[here, :] = (hidden[here, :] + r * (scaled - first - xhat * second)).astype(BF)
        vec_acc[0] += by_eight(dn * xhat)
        vec_acc[1] += by_eight(dn)
        tick(f"norm1.{i}")

    store_gtok = local(gtok_b, gtok_h, 7)

    tick("end")
    store_out.wait()
    store_gtok.wait()
    copies.drain()


def result_kernel(sizes, *refs):
    n_t, n_dp, hidden_w = sizes
    sources, vec, results, shares, sems = refs[:6], refs[6], refs[7:13], refs[13:20], refs[20]
    copies = [
        pltpu.make_async_copy(src, dst, sems.at[i])
        for i, (src, dst) in enumerate(zip(sources, results))
    ]
    for copy in copies:
        copy.start()
    d, t = lax.axis_index("dp"), lax.axis_index("tensor")
    width = vec.shape[1]
    first = (d * n_t + t) * (width // (n_dp * n_t))
    lines = pltpu.roll(vec[...], lax.rem(width - first, width), 1)
    for i in range(6):
        shares[i][...] = lines[i : i + 1, : shares[i].shape[1]]
    lines = pltpu.roll(vec[...], lax.rem(width - d * (hidden_w // n_dp), width), 1)
    shares[6][...] = lines[6:7, : shares[6].shape[1]]
    for copy in copies:
        copy.wait()


def fused_device(
    n_t,
    n_dp,
    tokens,
    clip_ids,
    ln1_gain,
    ln1_bias,
    query_key_value_weight,
    projection_weight,
    attention_output_bias,
    ln2_gain,
    ln2_bias,
    up_weight,
    mlp_up_bias,
    down_weight,
    mlp_down_bias,
    grad_output,
):
    _, rows, width = tokens.shape
    heads_w = projection_weight.shape[0]
    hidden_w = up_weight.shape[1]
    n_y, n_x, n_l, n_h = n_t // CORES, WIDE, PAIR, n_dp // (WIDE * PAIR)
    part = width // n_dp
    blocks = rows // BLOCK
    qkv_w = 3 * heads_w
    def chunk(tag, w):
        sizes = {"h": n_h, "l": n_l, "x": n_x}
        dims, early = ["h", "l", "x"], True
        bufs = [
            pltpu.VMEM((n_t, n_h, n_l, n_x, part, w), BF),
            pltpu.VMEM((n_y, n_h, n_l, n_x, part, w), BF),
        ]
        for axis in ORDER[tag]:
            if axis == "y":
                early = False
                lead = (n_y - 1,)
            else:
                dims = [a for a in dims if a != axis]
                lead = ((n_y,) if early else ()) + (sizes[axis] - 1,)
            bufs.append(pltpu.VMEM(lead + tuple(sizes[a] for a in dims) + (part, w), BF))
        return bufs

    def half(*shape):
        return pltpu.VMEM(shape, BF)

    def single(*shape):
        return pltpu.VMEM(shape, F32)

    scratch = [
        half(rows, width),
        half(rows, width),
        half(n_t, 3, width, heads_w),
        half(n_t, heads_w, width),
        half(n_t, width, hidden_w),
        half(n_t, hidden_w, width),
        single(n_t, 8, hidden_w),
        half(rows, width),
        single(4, rows, BLOCK),
        half(n_t, rows, heads_w),
        half(n_t, rows + BLOCK, heads_w),
        half(n_t, rows + BLOCK, heads_w),
        half(n_t, heads_w, rows + BLOCK),
        half(n_t, heads_w, rows + BLOCK),
        single(blocks, 2 * BLOCK, BLOCK),
        half(n_t, blocks, 2 * BLOCK, 2 * BLOCK),
        half(rows, n_t * heads_w),
        single(rows, width),
        half(rows, width),
        single(rows, width),
        single(rows, width),
        half(rows, hidden_w),
        half(rows, hidden_w),
        half(rows, width),
        half(rows, n_t * heads_w),
        half(rows, n_t * qkv_w),
        single(6, 8, width),
        single(n_t, 8, hidden_w),
        single(n_t, 8, width),
        single(n_t - 1, 8, width),
        single(8, width),
        single(n_dp - 1, 8, width),
        chunk("u", hidden_w),
        chunk("d", hidden_w),
        chunk("p", heads_w),
        chunk("qk", 2 * heads_w),
        chunk("v", heads_w),
        half(rows, width),
        half(rows, width),
        pltpu.SemaphoreType.DMA((8,)),
        pltpu.SemaphoreType.DMA((128,)),
        pltpu.SemaphoreType.DMA((128,)),
    ]
    anywhere = pl.BlockSpec(memory_space=pl.ANY)
    near = pl.BlockSpec(memory_space=pltpu.VMEM)
    results = pl.pallas_call(
        functools.partial(layer_kernel, (n_t, n_dp, rows, width, heads_w, hidden_w)),
        out_shape=(
            jax.ShapeDtypeStruct((rows, width), BF),
            jax.ShapeDtypeStruct((rows, width), BF),
            jax.ShapeDtypeStruct((3, part, heads_w), F32),
            jax.ShapeDtypeStruct((part, heads_w), F32),
            jax.ShapeDtypeStruct((part, hidden_w), F32),
            jax.ShapeDtypeStruct((part, hidden_w), F32),
            jax.ShapeDtypeStruct((8, width), F32),
        ),
        in_specs=[anywhere] * 2 + [near] * 8 + [anywhere] * 4,
        out_specs=[anywhere] * 2 + [near] * 5,
        scratch_shapes=scratch,
        compiler_params=pltpu.CompilerParams(
            collective_id=0, has_side_effects=True, vmem_limit_bytes=63 << 20
        ),
    )(
        tokens.reshape(rows, width),
        grad_output.reshape(rows, width),
        clip_ids,
        ln1_gain.reshape(1, width),
        ln1_bias.reshape(1, width),
        attention_output_bias.reshape(1, width),
        ln2_gain.reshape(1, width),
        ln2_bias.reshape(1, width),
        mlp_down_bias.reshape(1, width),
        mlp_up_bias.reshape(1, hidden_w),
        jnp.transpose(query_key_value_weight, (1, 0, 2)),
        projection_weight,
        up_weight,
        down_weight,
    )
    share = width // (n_dp * n_t)
    out, gtok, gq, gp, gu, gd, *vectors, g_up_bias = pl.pallas_call(
        functools.partial(result_kernel, (n_t, n_dp, hidden_w)),
        out_shape=[jax.ShapeDtypeStruct(r.shape, r.dtype) for r in results[:6]]
        + [jax.ShapeDtypeStruct((1, share), F32)] * 6
        + [jax.ShapeDtypeStruct((1, hidden_w // n_dp), F32)],
        in_specs=[near] * 7,
        out_specs=[anywhere] * 6 + [near] * 7,
        scratch_shapes=[pltpu.SemaphoreType.DMA((6,))],
    )(*results)
    vectors = [v.reshape(share) for v in vectors]
    return (
        out[None],
        gtok[None],
        vectors[0],
        vectors[1],
        jnp.transpose(gq, (1, 0, 2)),
        gp.T,
        vectors[2],
        vectors[3],
        vectors[4],
        gu,
        g_up_bias,
        gd.T,
        vectors[5],
    )


def fits(mesh, shapes):
    n_t, n_dp = mesh.shape["tensor"], mesh.shape["dp"]
    seqs, length, width = shapes[0]
    features = shapes[4][2] // n_t
    hidden_w = shapes[9][1] // n_t
    return (
        seqs == n_t * n_dp
        and length % ROWS == 0
        and features == 2 * HD == BLOCK
        and hidden_w == width
        and n_t % CORES == 0
        and n_t // CORES > 1
        and n_dp % (2 * WIDE) == 0
        and (width // n_dp) % 16 == 0
    )


def solution(mesh):
    in_specs = (
        P(("dp", "tensor"), None, None),
        P("dp", None),
        P(),
        P(),
        P(None, None, "tensor"),
        P("tensor", None),
        P(),
        P(),
        P(),
        P(None, "tensor"),
        P("tensor"),
        P("tensor", None),
        P(),
        P(("dp", "tensor"), None, None),
    )
    out_specs = (
        P(("dp", "tensor"), None, None),
        P(("dp", "tensor"), None, None),
        P(("dp", "tensor")),
        P(("dp", "tensor")),
        P("dp", None, "tensor"),
        P("tensor", "dp"),
        P(("dp", "tensor")),
        P(("dp", "tensor")),
        P(("dp", "tensor")),
        P("dp", "tensor"),
        P("tensor", "dp"),
        P("tensor", "dp"),
        P(("dp", "tensor")),
    )

    def run(*arrays):
        body = on_device
        if fits(mesh, [a.shape for a in arrays]):
            body = functools.partial(fused_device, mesh.shape["tensor"], mesh.shape["dp"])
        return jax.shard_map(
            body, mesh=mesh, in_specs=in_specs, out_specs=out_specs, check_vma=False
        )(*arrays)

    return run
```

```python
import functools
import math

import jax
import jax.numpy as jnp
from jax import lax
from jax.experimental import pallas as pl
from jax.experimental.pallas import tpu as pltpu
from jax.sharding import PartitionSpec as P

HD = 64
CORES = 2
WIDE = 2
PAIR = 2
BF = jnp.bfloat16
F32 = jnp.float32
MESH = pl.DeviceIdType.MESH


epsilon = 1e-05


def layer_norm(values, gain, shift):
    centre = values - jnp.mean(values, axis=-1, keepdims=True)
    spread = jnp.mean(centre * centre, axis=-1, keepdims=True)
    return centre * lax.rsqrt(spread + epsilon) * gain + shift


def gelu_exact(values):
    return jax.nn.gelu(values, approximate=False)


def visible(clip_row, start, count):
    length = clip_row.shape[0]
    query_pos = start + jnp.arange(count)
    key_pos = jnp.arange(length)
    query_clip = clip_row[start : start + count]
    return (key_pos[None, :] <= query_pos[:, None]) & (query_clip[:, None] == clip_row[None, :])


def block_scores(query, keys, clip_row, start, block):
    scale = query.shape[-1] ** (-0.5)
    allowed = visible(clip_row, start, block)
    scores = (
        jnp.einsum(
            "qhd,khd->hqk", query[start : start + block], keys, preferred_element_type=jnp.float32
        )
        * scale
    )
    return (jnp.where(allowed[None], scores, -1e30), allowed)


def attend_sequence(pieces):
    query, keys, vals, clip_row = pieces
    length = query.shape[0]
    block = min(512, length)
    outs = []
    sums = []
    for start in range(0, length, block):
        scores, allowed = block_scores(query, keys, clip_row, start, block)
        peak = jnp.max(scores, axis=-1, keepdims=True)
        expo = jnp.exp(scores - peak)
        total = jnp.sum(expo, axis=-1, keepdims=True)
        probs = (expo / total).astype(jnp.bfloat16)
        outs.append(jnp.einsum("hqk,khd->qhd", probs, vals, preferred_element_type=jnp.float32))
        sums.append((peak + jnp.log(total))[..., 0])
    return (jnp.concatenate(outs, 0), jnp.concatenate(sums, 1))


def attend_back(pieces):
    query, keys, vals, clip_row, lse, grad_mixed = pieces
    length = query.shape[0]
    block = min(512, length)
    scale = query.shape[-1] ** (-0.5)
    grad_keys = jnp.zeros(keys.shape, jnp.float32)
    grad_vals = jnp.zeros(vals.shape, jnp.float32)
    query_parts = []
    for start in range(0, length, block):
        scores, allowed = block_scores(query, keys, clip_row, start, block)
        probs_f = jnp.where(
            allowed[None], jnp.exp(scores - lse[:, start : start + block, None]), 0.0
        )
        probs = probs_f.astype(jnp.bfloat16)
        grad_block = grad_mixed[start : start + block]
        dprobs = jnp.einsum("qhd,khd->hqk", grad_block, vals, preferred_element_type=jnp.float32)
        grad_vals = grad_vals + jnp.einsum(
            "hqk,qhd->khd", probs, grad_block, preferred_element_type=jnp.float32
        )
        inner = jnp.sum(probs_f * dprobs, axis=-1, keepdims=True)
        dscores = (probs_f * (dprobs - inner)).astype(jnp.bfloat16)
        query_parts.append(
            jnp.einsum("hqk,khd->qhd", dscores, keys, preferred_element_type=jnp.float32) * scale
        )
        grad_keys = (
            grad_keys
            + jnp.einsum(
                "hqk,qhd->khd",
                dscores,
                query[start : start + block],
                preferred_element_type=jnp.float32,
            )
            * scale
        )
    return (jnp.concatenate(query_parts, 0), grad_keys, grad_vals)


def on_device(
    tokens,
    clip_ids,
    ln1_gain,
    ln1_bias,
    query_key_value_weight,
    projection_weight,
    attention_output_bias,
    ln2_gain,
    ln2_bias,
    up_weight,
    mlp_up_bias,
    down_weight,
    mlp_down_bias,
    grad_output,
):
    head_size = HD
    local_width = query_key_value_weight.shape[2]
    local_heads = local_width // head_size
    tok_f = tokens.astype(jnp.float32)
    first_normalized = layer_norm(tok_f, ln1_gain, ln1_bias).astype(jnp.bfloat16)
    first_normalized_every = lax.all_gather(first_normalized, "tensor", axis=0, tiled=True)
    seqs = first_normalized_every.shape[0]
    length = first_normalized_every.shape[1]
    query_key_value_rows = jnp.einsum(
        "tre,eub->trub",
        first_normalized_every,
        query_key_value_weight,
        preferred_element_type=jnp.float32,
    ).astype(jnp.bfloat16)
    query_key_value_rows = query_key_value_rows.reshape(seqs, length, 3, local_heads, head_size)
    query = query_key_value_rows[:, :, 0]
    keys = query_key_value_rows[:, :, 1]
    vals = query_key_value_rows[:, :, 2]
    mixed_heads_output, lse = lax.map(attend_sequence, (query, keys, vals, clip_ids))
    mixed_heads_lowered = mixed_heads_output.astype(jnp.bfloat16).reshape(seqs, length, local_width)
    attention_piece = jnp.einsum(
        "bne,eo->bno", mixed_heads_lowered, projection_weight, preferred_element_type=jnp.float32
    )
    attn_rows = lax.psum_scatter(
        attention_piece.astype(jnp.bfloat16), "tensor", scatter_dimension=0, tiled=True
    ).astype(jnp.float32)
    hidden_activation = tok_f + attn_rows + attention_output_bias
    second_normalized = layer_norm(hidden_activation, ln2_gain, ln2_bias).astype(jnp.bfloat16)
    second_normalized_every = lax.all_gather(second_normalized, "tensor", axis=0, tiled=True)
    upper_half_rows = (
        jnp.einsum(
            "wih,hm->wim", second_normalized_every, up_weight, preferred_element_type=jnp.float32
        )
        + mlp_up_bias
    )
    active_rows_now = gelu_exact(upper_half_rows).astype(jnp.bfloat16)
    perceptron_piece = jnp.einsum(
        "bne,eo->bno", active_rows_now, down_weight, preferred_element_type=jnp.float32
    )
    mlp_rows = lax.psum_scatter(
        perceptron_piece.astype(jnp.bfloat16), "tensor", scatter_dimension=0, tiled=True
    ).astype(jnp.float32)
    output = (hidden_activation + mlp_rows + mlp_down_bias).astype(jnp.bfloat16)
    gradient_every_row = lax.all_gather(grad_output, "tensor", axis=0, tiled=True)
    down_weight_gradient = jnp.einsum(
        "egz,egb->zb", active_rows_now, gradient_every_row, preferred_element_type=jnp.float32
    )
    gradient_active_rows = jnp.einsum(
        "etk,ok->eto", gradient_every_row, down_weight, preferred_element_type=jnp.float32
    )
    gradient_upper_half = jax.vjp(gelu_exact, upper_half_rows)[1](gradient_active_rows)[0].astype(
        jnp.bfloat16
    )
    g_up_bias = jnp.sum(gradient_upper_half, axis=(0, 1), dtype=jnp.float32)
    up_weight_gradient = jnp.einsum(
        "kjy,kjt->yt",
        second_normalized_every,
        gradient_upper_half,
        preferred_element_type=jnp.float32,
    )
    grad_normed2_part = jnp.einsum(
        "hwm,bm->hwb", gradient_upper_half, up_weight, preferred_element_type=jnp.float32
    )
    grad_normed2 = lax.psum_scatter(
        grad_normed2_part.astype(jnp.bfloat16), "tensor", scatter_dimension=0, tiled=True
    ).astype(jnp.float32)
    grad_hidden_ln, g_ln2_gain, g_ln2_bias = jax.vjp(
        layer_norm, hidden_activation, ln2_gain, ln2_bias
    )[1](grad_normed2)
    grad_f = grad_output.astype(jnp.float32)
    grad_hidden = grad_f + grad_hidden_ln
    g_down_bias = jnp.sum(grad_f, axis=(0, 1))
    g_proj_bias = jnp.sum(grad_hidden, axis=(0, 1))
    branch_low = grad_hidden.astype(jnp.bfloat16)
    branch_every_row = lax.all_gather(branch_low, "tensor", axis=0, tiled=True)
    projection_weight_gradient = jnp.einsum(
        "egz,egb->zb", mixed_heads_lowered, branch_every_row, preferred_element_type=jnp.float32
    )
    grad_mixed = jnp.einsum(
        "etk,ok->eto", branch_every_row, projection_weight, preferred_element_type=jnp.float32
    ).astype(jnp.bfloat16)
    grad_mixed = grad_mixed.reshape(seqs, length, local_heads, head_size)
    grad_query, grad_keys, grad_vals = lax.map(
        attend_back, (query, keys, vals, clip_ids, lse, grad_mixed)
    )
    gradient_query_key_value = (
        jnp.stack((grad_query, grad_keys, grad_vals), axis=2)
        .astype(jnp.bfloat16)
        .reshape(seqs, length, 3, local_width)
    )
    query_key_value_gradient = jnp.einsum(
        "zny,znqj->yqj",
        first_normalized_every,
        gradient_query_key_value,
        preferred_element_type=jnp.float32,
    )
    grad_normed_part = jnp.einsum(
        "kegu,hgu->keh",
        gradient_query_key_value,
        query_key_value_weight,
        preferred_element_type=jnp.float32,
    )
    grad_normed = lax.psum_scatter(
        grad_normed_part.astype(jnp.bfloat16), "tensor", scatter_dimension=0, tiled=True
    ).astype(jnp.float32)
    grad_tok_ln, g_ln1_gain, g_ln1_bias = jax.vjp(layer_norm, tok_f, ln1_gain, ln1_bias)[1](
        grad_normed
    )
    grad_tokens = (grad_hidden + grad_tok_ln).astype(jnp.bfloat16)
    g_qkv_s, g_proj_s, g_up_s, g_up_bias_s, g_down_s = (
        lax.psum_scatter(
            query_key_value_gradient.astype(jnp.bfloat16), "dp", scatter_dimension=0, tiled=True
        ).astype(jnp.float32),
        lax.psum_scatter(
            projection_weight_gradient.astype(jnp.bfloat16), "dp", scatter_dimension=1, tiled=True
        ).astype(jnp.float32),
        lax.psum_scatter(
            up_weight_gradient.astype(jnp.bfloat16), "dp", scatter_dimension=0, tiled=True
        ).astype(jnp.float32),
        lax.psum_scatter(
            g_up_bias[None].astype(jnp.bfloat16), "dp", scatter_dimension=1, tiled=True
        ).astype(jnp.float32),
        lax.psum_scatter(
            down_weight_gradient.astype(jnp.bfloat16), "dp", scatter_dimension=1, tiled=True
        ).astype(jnp.float32),
    )
    v_ln1_gain, v_ln1_bias, v_proj_bias, v_ln2_gain, v_ln2_bias, v_down_bias = (
        lax.psum_scatter(g_ln1_gain, ("dp", "tensor"), scatter_dimension=0, tiled=True),
        lax.psum_scatter(g_ln1_bias, ("dp", "tensor"), scatter_dimension=0, tiled=True),
        lax.psum_scatter(g_proj_bias, ("dp", "tensor"), scatter_dimension=0, tiled=True),
        lax.psum_scatter(g_ln2_gain, ("dp", "tensor"), scatter_dimension=0, tiled=True),
        lax.psum_scatter(g_ln2_bias, ("dp", "tensor"), scatter_dimension=0, tiled=True),
        lax.psum_scatter(g_down_bias, ("dp", "tensor"), scatter_dimension=0, tiled=True),
    )
    return (
        output,
        grad_tokens,
        v_ln1_gain,
        v_ln1_bias,
        g_qkv_s,
        g_proj_s,
        v_proj_bias,
        v_ln2_gain,
        v_ln2_bias,
        g_up_s,
        g_up_bias_s,
        g_down_s,
        v_down_bias,
    )


BLOCK = 128
ROWS = 256
WIDE_ROWS = 512
PARTS = 4
AXES = {"x": ("x",), "l": ("l",), "h": ("h",), "w": ("l", "x"), "z": ("h", "l")}
SOON = ("wq",)

ORDER = {"u": "xlg", "d": "lxg", "qk": "xlg", "pv": "ywh"}
SCHEDULE = {
    "start": ("wp", "wq", "wu", "wd",),
    "heads0": ("wp",),
    "attend0": ("wq",),
    "attend1": ("wp", "wq", "wq",),
    "dact": ("wp", "wu",),
    "attend2": ("wd",),
    "hidden": ("wu",),
    "rows1.1": ("wd",),
    "mlp1": ("d0",),
    "rows0.0": ("wu", "u0",),
    "rows0.1": ("wd",),
    "mlp0": ("u0", "d0",),
    "mlp3": ("u1", "d1",),
    "mlp2": ("d1", "u1", "u0",),
    "qkv3": ("d0", "qk1", "pv1",),
    "qkv2": ("qk1", "u1", "pv1",),
    "qkv1": ("u0", "d0", "qk0", "d1",),
    "qkv0": ("qk1", "u1", "pv0", "qk0",),
    "norm1.0": ("pv0", "pv",),
    "norm1.1": ("vec", "d1",),
    "out.0": ("qk0", "qk1", "u", "vec", "pv",),
    "out.1": ("qk0", "vec",),
    "end": ("d", "pv", "qk",),
}


def mm(left, right):
    return lax.dot_general(left, right, (((1,), (0,)), ((), ())), preferred_element_type=F32)


def mm_nt(left, right):
    return lax.dot_general(left, right, (((1,), (1,)), ((), ())), preferred_element_type=F32)


def mm_tn(left, right):
    return lax.dot_general(left, right, (((0,), (0,)), ((), ())), preferred_element_type=F32)


def normal_parts(u):
    cdf = 0.5 + 0.5 * lax.erf(u * math.sqrt(0.5))
    bell = jnp.exp2(u * u * (-0.5 * math.log2(math.e)))
    return cdf, u * bell * (1.0 / math.sqrt(2.0 * math.pi))


def by_eight(values):
    return jnp.sum(values.reshape(-1, 8, values.shape[-1]), axis=0)


class Copies:
    def __init__(self, send, recv):
        self.send, self.recv, self.made, self.started = send, recv, {}, []

    def describe(self, name, src, dst, device):
        at = self.made.setdefault(name, len(self.made))
        return pltpu.make_async_remote_copy(
            src_ref=src,
            dst_ref=dst,
            send_sem=self.send.at[at],
            recv_sem=self.recv.at[at],
            device_id=device,
            device_id_type=MESH,
        )

    def start(self, name, src, dst, device):
        copy = self.describe(name, src, dst, device)
        copy.start()
        self.started.append(copy)

    def arrived(self, name, dst, device):
        self.describe(name, dst, dst, device).wait_recv()

    def drain(self):
        for copy in self.started:
            copy.wait_send()


def layer_kernel(
    sizes,
    tok_h,
    dy_h,
    clip_ref,
    ln1_gain_ref,
    ln1_bias_ref,
    proj_bias_ref,
    ln2_gain_ref,
    ln2_bias_ref,
    down_bias_ref,
    bu_ref,
    wq_h,
    wp_h,
    wu_h,
    wd_h,
    out_h,
    gtok_h,
    gq_ref,
    gp_ref,
    gu_ref,
    gd_ref,
    gv_ref,
    tok,
    dy,
    wq,
    wp,
    wu,
    wd,
    bu,
    n1,
    stats,
    qs,
    ks,
    vs,
    ks_t,
    vs_t,
    bias,
    probs,
    mixed,
    hidden,
    n2,
    dn2_acc,
    act,
    dact,
    dup,
    branch,
    dmixed,
    dtri,
    vec_acc,
    bup_acc,
    vec_mine,
    vec_t,
    vec_sum,
    vec_dp,
    u_bufs,
    d_bufs,
    qk_bufs,
    pv_bufs,
    out_b,
    gtok_b,
    local_sem,
    send_sem,
    recv_sem,
):
    n_t, n_dp, rows, width, heads_w, hidden_w = sizes
    n_y, n_x, n_l, n_h = n_t // CORES, WIDE, PAIR, n_dp // (WIDE * PAIR)
    blocks = rows // BLOCK
    part = width // n_dp
    qkv_w = 3 * heads_w
    d, t = lax.axis_index("dp"), lax.axis_index("tensor")
    y, c = t // CORES, lax.rem(t, CORES)
    z, x = d // WIDE, lax.rem(d, WIDE)
    z_far, z_near = z // n_l, lax.rem(z, n_l)

    def t_peer(dy_, dc_):
        return (d, lax.rem(y + dy_, n_y) * CORES + lax.rem(c + dc_, CORES))

    def x_peer(k):
        return (z * WIDE + lax.rem(x + k, n_x), t)

    def dp_peer(h_off, l_off, x_off):
        far, near = lax.rem(z_far + h_off, n_h), lax.rem(z_near + l_off, n_l)
        return ((far * n_l + near) * WIDE + lax.rem(x + x_off, n_x), t)

    def l_peer(k):
        return dp_peer(0, k, 0)

    peers = [t_peer(s // CORES, s % CORES) for s in range(1, n_t)]
    peers += [(lax.rem(d + k, n_dp), t) for k in range(1, n_dp)]
    for k in range(1, n_y):
        for h in range(1, n_h):
            peers.append((dp_peer(h, 0, 0)[0], t_peer(k, 0)[1]))
    core = t_peer(0, 1)

    barrier = pltpu.get_barrier_semaphore()
    for peer in peers:
        pl.semaphore_signal(barrier, inc=1, device_id=peer, device_id_type=MESH)

    def local(src, dst, at):
        copy = pltpu.make_async_copy(src, dst, local_sem.at[at])
        copy.start()
        return copy

    load_tok = local(tok_h, tok, 0)
    load_wq = local(wq_h, wq.at[0], 1)
    load_wp = local(wp_h, wp.at[0], 2)
    load_dy = local(dy_h, dy, 3)
    load_wu = local(wu_h, wu.at[0], 4)
    load_wd = local(wd_h, wd.at[0], 5)
    bu[0] = jnp.broadcast_to(bu_ref[...], bu.shape[1:])

    ln1_gain, ln1_bias = ln1_gain_ref[...], ln1_bias_ref[...]
    proj_bias = proj_bias_ref[...]
    ln2_gain, ln2_bias = ln2_gain_ref[...], ln2_bias_ref[...]
    down_bias = down_bias_ref[...]
    vec_acc[...] = jnp.zeros_like(vec_acc)
    bup_acc[...] = jnp.zeros_like(bup_acc)

    clip = clip_ref[pl.ds(t, 1), :].astype(F32)
    key_at = lax.broadcasted_iota(jnp.int32, (BLOCK, BLOCK), 0)
    query_at = lax.broadcasted_iota(jnp.int32, (BLOCK, BLOCK), 1)
    before = jnp.full((BLOCK, BLOCK), -1.0, F32)
    for i in range(blocks):
        row = clip[:, i * BLOCK : (i + 1) * BLOCK]
        ids = jnp.broadcast_to(row, (BLOCK, BLOCK))
        down = ids.T
        bias[i, 0:BLOCK, :] = jnp.where(before == ids, 0.0, -1e30)
        bias[i, BLOCK:, :] = jnp.where((down == ids) & (key_at <= query_at), 0.0, -1e30)
        before = down

    for s in range(n_t):
        ks[s, 0:BLOCK, :] = jnp.zeros((BLOCK, heads_w), BF)
        vs[s, 0:BLOCK, :] = jnp.zeros((BLOCK, heads_w), BF)
        ks_t[s, :, 0:BLOCK] = jnp.zeros((heads_w, BLOCK), BF)
        vs_t[s, :, 0:BLOCK] = jnp.zeros((heads_w, BLOCK), BF)

    def at(i, size, offset=0):
        return pl.ds(pl.multiple_of(i * size + offset, math.gcd(size, offset) if offset else size), size)

    load_tok.wait()

    @pl.loop(0, rows // ROWS)
    def _(i):
        here = at(i, ROWS)
        v = tok[here, :].astype(F32)
        mean = jnp.mean(v, axis=-1, keepdims=True)
        centre = v - mean
        r = lax.rsqrt(jnp.mean(centre * centre, axis=-1, keepdims=True) + epsilon)
        normed = (centre * r * ln1_gain + ln1_bias).astype(BF)
        n1[here, :] = normed
        stats[0, here, :] = jnp.broadcast_to(mean, (ROWS, BLOCK))
        stats[1, here, :] = jnp.broadcast_to(r, (ROWS, BLOCK))

    pl.semaphore_wait(barrier, len(peers))
    copies = Copies(send_sem, recv_sem)

    full = {"wq": (wq_h, wq), "wp": (wp_h, wp), "wu": (wu_h, wu), "wd": (wd_h, wd)}

    def rows_of(ref, which, parts):
        part = ref.shape[-2] // parts
        here = pl.ds(pl.multiple_of(which * part, part), part)
        return ref.at[:, here] if len(ref.shape) == 3 else ref.at[here]

    def gather(name):
        src, dst = full[name]
        quarters, mine = n_x * n_l, x * n_l + z_near
        across, along = lax.rem(x + 1, n_x) * n_l + z_near, x * n_l + lax.rem(z_near + 1, n_l)
        last = lax.rem(x + 1, n_x) * n_l + lax.rem(z_near + 1, n_l)

        def spot(k, which, halves=1, half=0):
            return rows_of(dst.at[CORES * k], which * halves + half, quarters * halves)

        def pass_on(k, n):
            which = (mine, across, along, last)[n]
            there = rows_of(dst.at[CORES * k + 1], which, quarters)
            copies.start((name, "core", k, n), spot(k, which), there, core)

        far = range(1, n_y)
        copies.start((name, "core", 0), src, dst.at[1], core)
        for k in far:
            copies.start(
                (name, "y", k), rows_of(src, mine, quarters), spot(k, mine), t_peer(n_y - k, 0)
            )
        yield
        for k in far:
            copies.arrived((name, "y", k), spot(k, mine), core)
            copies.start((name, "x", k), spot(k, mine), spot(k, mine), x_peer(1))
            copies.start((name, "l", k), spot(k, mine), spot(k, mine), l_peer(1))
            pass_on(k, 0)
        yield
        for k in far:
            copies.arrived((name, "x", k), spot(k, across), core)
            first = spot(k, across, 2, 0)
            copies.start((name, "xl", k), first, first, l_peer(1))
            copies.arrived((name, "l", k), spot(k, along), core)
            second = spot(k, along, 2, 1)
            copies.start((name, "lx", k), second, second, x_peer(1))
            pass_on(k, 1)
            pass_on(k, 2)
        yield
        for k in far:
            copies.arrived((name, "xl", k), spot(k, last, 2, 0), core)
            copies.arrived((name, "lx", k), spot(k, last, 2, 1), core)
            pass_on(k, 3)
        yield

    def gather_soon(name):
        src, dst = full[name]
        parts = 2 * n_x
        far = range(1, n_y)

        def spot(k, which, whole_half=False):
            if whole_half:
                return rows_of(dst.at[k], 1, 2)
            return rows_of(dst.at[k], which, parts)

        copies.start((name, "core", 0), src, dst.at[1], core)
        for k in far:
            peer = t_peer(n_y - k, 0)
            copies.start((name, "y", k), rows_of(src, x, parts), spot(CORES * k, x), peer)
        for k in far:
            peer = t_peer(n_y - k, 0)
            second = spot(CORES * k, 0, True)
            copies.start((name, "yy", k), rows_of(src, 1, 2), second, peer)
        yield
        for k in far:
            got = spot(CORES * k, x)
            copies.arrived((name, "y", k), got, core)
            for j in range(1, n_x):
                copies.start((name, "x", k, j), got, got, x_peer(j))
            copies.start((name, "core", k, 0), got, spot(CORES * k + 1, x), core)
        yield
        for k in far:
            got = spot(CORES * k, 0, True)
            copies.arrived((name, "yy", k), got, core)
            copies.start((name, "core", k, n_x), got, spot(CORES * k + 1, 0, True), core)
        yield
        for k in far:
            for j in range(1, n_x):
                which = lax.rem(x + n_x - j, n_x)
                got = spot(CORES * k, which)
                copies.arrived((name, "x", k, j), got, core)
                copies.start((name, "core", k, j), got, spot(CORES * k + 1, which), core)
        yield

    def whole(name, s):
        _, dst = full[name]
        quarters = n_x * n_l
        if s == 1:
            copies.arrived((name, "core", 0), dst.at[1], core)
        elif s % CORES == 1 and name in SOON:
            for j in range(n_x):
                got = rows_of(dst.at[s], lax.rem(x + n_x - j, n_x), 2 * n_x)
                copies.arrived((name, "core", s // CORES, j), got, core)
            copies.arrived((name, "core", s // CORES, n_x), rows_of(dst.at[s], 1, 2), core)
        elif s % CORES == 1:
            here, there = lax.rem(x + 1, n_x) * n_l, lax.rem(z_near + 1, n_l)
            spots = [x * n_l + z_near, here + z_near, x * n_l + there, here + there]
            for n, which in enumerate(spots):
                got = rows_of(dst.at[s], which, quarters)
                copies.arrived((name, "core", s // CORES, n), got, core)

    position = {"x": x, "l": z_near, "h": z_far}
    extent = {"x": n_x, "l": n_l, "h": n_h}
    reduced = {}

    def steps_along(group):
        offsets = [{}]
        for axis in group:
            offsets = [dict(o, **{axis: k}) for o in offsets for k in range(extent[axis])]
        return [o for o in offsets if any(o.values())]

    def part_for(dims, group, offset):
        return tuple(
            lax.rem(position[a] + offset[a], extent[a]) if a in group else slice(None) for a in dims
        )

    def spots_of(dims):
        spots = [()]
        for axis in dims:
            spots = [spot + (a,) for spot in spots for a in range(extent[axis])]
        return spots

    def sum_f32(values):
        return functools.reduce(lambda a, b: a + b, [v.astype(F32) for v in values])

    def send_parts(name, cur, dims, step, recv):
        group = AXES[step]
        for j, offset in enumerate(steps_along(group)):
            peer = dp_peer(*(offset.get(a, 0) for a in ("h", "l", "x")))
            copies.start(
                (name, step, j), cur.at[part_for(dims, group, offset)], recv.at[j], peer
            )

    def fold(name, cur, dims, step, recv, keep=True):
        group = AXES[step]
        others = len(steps_along(group))
        for j in range(others):
            copies.arrived((name, step, j), recv.at[j], core)
        rest = [a for a in dims if a not in group]
        total = None
        for spot in spots_of(rest):
            at_rest = dict(zip(rest, spot))
            mine = cur[tuple(position[a] if a in group else at_rest[a] for a in dims)]
            total = sum_f32([mine] + [recv[(j,) + spot] for j in range(others)])
            if keep:
                recv[(0,) + spot] = total.astype(BF)
        return (recv.at[0] if keep else total), rest

    def reduce_pair(tag, bufs, k):
        order = ORDER[tag]
        at_y = max(order.find("y"), order.find("g"))
        own, got = bufs[:2]
        copies.start((tag, "core", k), own.at[CORES * k + 1], got.at[k], core)
        yield
        copies.arrived((tag, "core", k), got.at[k], core)
        for spot in spots_of(["h", "l", "x"]):
            here = (CORES * k,) + spot
            own[here] = own[here] + got[(k,) + spot]
        cur, dims = own.at[CORES * k], ["h", "l", "x"]
        for n, step in enumerate(order[: at_y]):
            recv = bufs[2 + n].at[k]
            send_parts((tag, k), cur, dims, step, recv)
            yield
            cur, dims = fold((tag, k), cur, dims, step, recv)
        if order[at_y] == "g":
            recv = bufs[-1]
            for off in range(n_h):
                if k or off:
                    mine = cur.at[part_for(dims, ("h",), {"h": off})]
                    peer = (dp_peer(off, 0, 0)[0], t_peer(k, 0)[1])
                    copies.start((tag, "g", k, off), mine, recv.at[k, off], peer)
        elif k > 0:
            copies.start((tag, "y", k), cur, bufs[2 + at_y].at[k - 1], t_peer(k, 0))
        reduced[tag, k] = cur, dims
        yield

    def reduce_end(tag, bufs, write):
        order = ORDER[tag]
        cur, dims = reduced[tag, 0]
        at_y = order.find("y")
        if at_y < 0:
            terms = [cur[z_far]]
            for k in range(n_y):
                for off in range(n_h):
                    if k or off:
                        copies.arrived((tag, "g", k, off), bufs[-1].at[k, off], core)
                        terms.append(bufs[-1][k, off])
            write(sum_f32(terms))
            yield
            return
        recv = bufs[2 + at_y]
        for k in range(1, n_y):
            copies.arrived((tag, "y", k), recv.at[k - 1], core)
        total = None
        for spot in spots_of(dims):
            total = sum_f32([cur[spot]] + [recv[(k,) + spot] for k in range(n_y - 1)])
            if dims:
                recv[(0,) + spot] = total.astype(BF)
        cur = recv.at[0]
        for n, step in enumerate(order[at_y + 1 :]):
            recv = bufs[3 + at_y + n]
            send_parts(tag, cur, dims, step, recv)
            yield
            cur, dims = fold(tag, cur, dims, step, recv, at_y + 2 + n < len(order))
            total = cur
        write(total)
        yield

    def write_up(total):
        gu_ref[...] = total

    def write_down(total):
        gd_ref[...] = total

    def write_query_key(total):
        gq_ref[0] = total[:, :heads_w]
        gq_ref[1] = total[:, heads_w:]

    def write_proj_value(total):
        gp_ref[...] = total[:, :heads_w]
        gq_ref[2] = total[:, heads_w:]

    def lanes_of(who):
        return pl.ds(pl.multiple_of(who * (width // n_dp) // BLOCK * BLOCK, BLOCK), BLOCK)

    def vectors():
        for s in range(n_t):
            lines = [jnp.sum(vec_acc[k], axis=0, keepdims=True) for k in range(6)]
            lines.append(jnp.sum(bup_acc[s], axis=0, keepdims=True))
            lines.append(jnp.zeros((1, width), F32))
            vec_mine[s] = jnp.concatenate(lines, axis=0)
        for s in range(1, n_t):
            copies.start(("vt", s), vec_mine.at[s], vec_t.at[s - 1], t_peer(s // CORES, s % CORES))
        yield
        total = vec_mine[0]
        for s in range(1, n_t):
            copies.arrived(("vt", s), vec_t.at[s - 1], core)
            total = total + vec_t[s - 1]
        vec_sum[...] = total
        for k in range(1, n_dp):
            peer = lax.rem(d + k, n_dp)
            copies.start(("vd", k), vec_sum.at[:, lanes_of(peer)], vec_dp.at[k - 1], (peer, t))
        yield
        total = vec_sum[:, lanes_of(d)]
        for k in range(1, n_dp):
            copies.arrived(("vd", k), vec_dp.at[k - 1], core)
            total = total + vec_dp[k - 1]
        gv_ref[...] = total
        yield

    u_own, d_own, qk_own, pv_own = u_bufs[0], d_bufs[0], qk_bufs[0], pv_bufs[0]
    sums = {
        "u": (u_bufs, write_up),
        "d": (d_bufs, write_down),
        "qk": (qk_bufs, write_query_key),
        "pv": (pv_bufs, write_proj_value),
    }
    steps = {name: gather_soon(name) if name in SOON else gather(name) for name in full}
    for tag, (bufs, write) in sums.items():
        for k in range(n_y):
            steps[tag + str(k)] = reduce_pair(tag, bufs, k)
        steps[tag] = reduce_end(tag, bufs, write)
    steps["vec"] = vectors()

    def tick(name):
        for step in SCHEDULE.get(name, ()):
            next(steps[step])

    tick("start")
    for s in range(1, n_t):
        copies.start(
            ("bu", s),
            bu.at[0],
            bu.at[s],
            t_peer((n_y - s // CORES) % n_y, (CORES - s % CORES) % CORES),
        )

    first_head = lax.broadcasted_iota(jnp.int32, (BLOCK, heads_w), 1) < HD

    def two_heads(block):
        zero = jnp.zeros_like(block)
        return jnp.concatenate(
            [jnp.where(first_head, block, zero), jnp.where(first_head, zero, block)], axis=0
        )

    def pick_heads(both):
        own = jnp.concatenate([both[:HD, :BLOCK], both[HD:, BLOCK:]], axis=0)
        return own.T

    def qkv_weight(slots):
        return jnp.concatenate([wq[s, j] for s in slots for j in range(3)], axis=1)

    def project_heads(slots):
        @pl.loop(0, rows // WIDE_ROWS)
        def _(i):
            here = at(i, WIDE_ROWS)
            there = at(i, WIDE_ROWS, BLOCK)
            all_of = mm(n1[here, :], qkv_weight(slots)).astype(BF)
            for n, s in enumerate(slots):
                got = all_of[:, n * qkv_w : (n + 1) * qkv_w]
                qs[s, here, :] = got[:, :heads_w] * jnp.asarray(HD**-0.5, BF)
                k = got[:, heads_w : 2 * heads_w]
                v = got[:, 2 * heads_w :]
                ks[s, there, :] = k
                vs[s, there, :] = v
                ks_t[s, :, there] = k.T
                vs_t[s, :, there] = v.T

    heres = [pl.ds(i * BLOCK, BLOCK) for i in range(blocks)]
    seens = [pl.ds(i * BLOCK, 2 * BLOCK) for i in range(blocks)]

    def attend_slot(s):
        scores = [
            mm_nt(ks[s, seen, :], two_heads(qs[s, here, :])) for here, seen in zip(heres, seens)
        ]
        lows = []
        for i in range(blocks):
            one = bias[i]
            score = scores[i] + jnp.concatenate([one, one], axis=1)
            expo = jnp.exp(score - jnp.max(score, axis=0, keepdims=True))
            total = jnp.sum(expo, axis=0, keepdims=True)
            low = (expo * (1.0 / total)).astype(BF)
            probs[s, i] = low
            lows.append(low)
        both = [mm(vs_t[s, :, seen], low) for seen, low in zip(seens, lows)]
        for i in range(blocks):
            mixed[heres[i], s * heads_w : (s + 1) * heads_w] = pick_heads(both[i]).astype(BF)

    load_wq.wait()
    whole("wq", 1)
    project_heads((0, 1))
    tick("heads0")
    attend_slot(0)
    tick("attend0")
    attend_slot(1)
    tick("attend1")
    load_dy.wait()
    load_wd.wait()
    dact[0] = mm_nt(dy[...], wd[0]).astype(BF)
    whole("wd", 1)
    dact[1] = mm_nt(dy[...], wd[1]).astype(BF)
    tick("dact")
    for k in range(1, n_y):
        slots = (CORES * k, CORES * k + 1)
        whole("wq", slots[0])
        whole("wq", slots[1])
        project_heads(slots)
        tick(f"heads{slots[0]}")
        for s in slots:
            attend_slot(s)
            tick(f"attend{s}")

    load_wp.wait()
    for s in range(1, n_t):
        whole("wp", s)

    @pl.loop(0, rows // ROWS)
    def _(i):
        here = at(i, ROWS)
        v = tok[here, :].astype(F32) + proj_bias
        v = v + mm(mixed[here, :], wp[...].reshape(n_t * heads_w, width))
        hidden[here, :] = v
        mean = jnp.mean(v, axis=-1, keepdims=True)
        centre = v - mean
        r = lax.rsqrt(jnp.mean(centre * centre, axis=-1, keepdims=True) + epsilon)
        normed = (centre * r * ln2_gain + ln2_bias).astype(BF)
        n2[here, :] = normed
        stats[2, here, :] = jnp.broadcast_to(mean, (ROWS, BLOCK))
        stats[3, here, :] = jnp.broadcast_to(r, (ROWS, BLOCK))

    tick("hidden")

    def mlp_slot(s, new):
        lanes = slice(s * hidden_w, (s + 1) * hidden_w)
        for i in range(rows // WIDE_ROWS):
            here = pl.ds(i * WIDE_ROWS, WIDE_ROWS)
            u = mm(n2[here, :], wu[s]) + bu[s, 0:1, :]
            back = dact[s, here, :] if s < CORES else mm_nt(dy[here, :], wd[s])
            cdf, bell = normal_parts(u)
            act[here, lanes] = (u * cdf).astype(BF)
            du = (back * (cdf + bell)).astype(BF)
            dup[here, :] = du
            bup_acc[s] += by_eight(du.astype(F32))
            back_part = mm_nt(du, wu[s])
            if new:
                dn2_acc[here, :] = back_part
            else:
                dn2_acc[here, :] += back_part
            tick(f"rows{s}.{i}")
        split = (n_h, n_l, n_x, part, hidden_w)
        u_own[s] = mm_tn(n2[...], dup[...]).astype(BF).reshape(split)
        d_own[s] = mm_tn(dy[...], act[:, lanes]).astype(BF).reshape(split)
        tick(f"mlp{s}")

    load_wu.wait()
    for s in range(1, n_t):
        copies.arrived(("bu", s), bu.at[s], core)
    order = [s + 1 - 2 * (s % CORES) for s in range(n_t)]
    for s in order:
        whole("wu", s)
        if s != 1:
            whole("wd", s)
        mlp_slot(s, s == order[0])

    for i in range(rows // WIDE_ROWS):
        here = pl.ds(i * WIDE_ROWS, WIDE_ROWS)
        value = hidden[here, :]
        mean = stats[2, here, 0:1]
        r = stats[3, here, 0:1]
        xhat = (value - mean) * r
        dn = dn2_acc[here, :]
        g = dy[here, :].astype(F32)
        scaled = dn * ln2_gain
        first = jnp.mean(scaled, axis=-1, keepdims=True)
        second = jnp.mean(scaled * xhat, axis=-1, keepdims=True)
        dh = g + r * (scaled - first - xhat * second)
        dn2_acc[here, :] = dh
        low = dh.astype(BF)
        branch[here, :] = low
        dmixed[here, :] = mm_nt(low, wp[...].reshape(n_t * heads_w, width)).astype(BF)
        vec_acc[2] += by_eight(dh)
        vec_acc[3] += by_eight(dn * xhat)
        vec_acc[4] += by_eight(dn)
        vec_acc[5] += by_eight(g)
        tick(f"norm2.{i}")

    got = mm_tn(branch[...], mixed[...]).astype(BF)
    for s in range(n_t):
        pv_own[s, :, :, :, :, :heads_w] = got[:, s * heads_w : (s + 1) * heads_w].reshape(
            n_h, n_l, n_x, part, heads_w
        )
    tick("proj")

    def attend_back_slot(s):
        lanes = slice(s * heads_w, (s + 1) * heads_w)
        first = s * qkv_w
        grads = [two_heads(dmixed[here, lanes]) for here in heres]
        dprobs = [mm_nt(vs[s, seen, :], grad) for seen, grad in zip(seens, grads)]
        ds = []
        for i in range(blocks):
            p = probs[s, i].astype(F32)
            weighed = p * dprobs[i]
            ds.append((weighed - p * jnp.sum(weighed, axis=0, keepdims=True)).astype(BF))
        dv = [mm(probs[s, i], grads[i]) for i in range(blocks)]
        dk = [mm(ds[i], two_heads(qs[s, heres[i], :])) for i in range(blocks)]
        dq = [pick_heads(mm(ks_t[s, :, seens[i]], ds[i])) * (HD**-0.5) for i in range(blocks)]
        for i in range(blocks):
            k_sum, v_sum = dk[i][BLOCK:], dv[i][BLOCK:]
            if i + 1 < blocks:
                k_sum, v_sum = k_sum + dk[i + 1][:BLOCK], v_sum + dv[i + 1][:BLOCK]
            dtri[heres[i], first : first + heads_w] = dq[i].astype(BF)
            dtri[heres[i], first + heads_w : first + 2 * heads_w] = k_sum.astype(BF)
            dtri[heres[i], first + 2 * heads_w : first + qkv_w] = v_sum.astype(BF)
        tick(f"back{s}")
        got = mm_tn(n1[...], dtri[:, first : first + qkv_w]).astype(BF)
        qk_own[s] = got[:, : 2 * heads_w].reshape(n_h, n_l, n_x, part, 2 * heads_w)
        pv_own[s, :, :, :, :, heads_w:] = got[:, 2 * heads_w :].reshape(
            n_h, n_l, n_x, part, heads_w
        )
        tick(f"qkv{s}")

    for s in reversed(range(n_t)):
        attend_back_slot(s)

    for i in range(rows // WIDE_ROWS):
        here = pl.ds(i * WIDE_ROWS, WIDE_ROWS)
        dn = mm_nt(dtri[here, :], qkv_weight(range(n_t)))
        mean = stats[0, here, 0:1]
        r = stats[1, here, 0:1]
        xhat = (tok[here, :].astype(F32) - mean) * r
        scaled = dn * ln1_gain
        first = jnp.mean(scaled, axis=-1, keepdims=True)
        second = jnp.mean(scaled * xhat, axis=-1, keepdims=True)
        gtok_b[here, :] = (dn2_acc[here, :] + r * (scaled - first - xhat * second)).astype(BF)
        vec_acc[0] += by_eight(dn * xhat)
        vec_acc[1] += by_eight(dn)
        tick(f"norm1.{i}")

    store_gtok = local(gtok_b, gtok_h, 7)

    for i in range(rows // WIDE_ROWS):
        here = pl.ds(i * WIDE_ROWS, WIDE_ROWS)
        grown = mm(act[here, :], wd[...].reshape(n_t * hidden_w, width))
        out_b[here, :] = (hidden[here, :] + grown + down_bias).astype(BF)
        tick(f"out.{i}")

    store_out = local(out_b, out_h, 6)

    tick("end")
    store_out.wait()
    store_gtok.wait()
    copies.drain()


def result_kernel(sizes, *refs):
    n_t, n_dp, width = sizes
    sources, vec, results, shares = refs[:6], refs[6], refs[7:13], refs[13:20]
    near, in_sems, out_sems = refs[20:26], refs[26], refs[27]
    pieces = []
    for src, mid, dst in zip(sources, near, results):
        parts = PARTS if src.shape[0] % (PARTS * ROWS) == 0 else 1
        step = src.shape[0] // parts
        for i in range(parts):
            here, at = pl.ds(i * step, step), len(pieces)
            coming = pltpu.make_async_copy(src.at[here], mid.at[here], in_sems.at[at])
            going = pltpu.make_async_copy(mid.at[here], dst.at[here], out_sems.at[at])
            coming.start()
            pieces.append((coming, going))
    for coming, going in pieces:
        coming.wait()
        going.start()
    d, t = lax.axis_index("dp"), lax.axis_index("tensor")
    first = lax.rem(d * (width // n_dp), BLOCK)
    lines = pltpu.roll(vec[...], lax.rem(BLOCK - first, BLOCK), 1)
    shares[6][...] = lines[6:7, : shares[6].shape[1]]
    first = first + t * (width // (n_dp * n_t))
    lines = pltpu.roll(vec[...], lax.rem(BLOCK - first, BLOCK), 1)
    for i in range(6):
        shares[i][...] = lines[i : i + 1, : shares[i].shape[1]]
    for _, going in pieces:
        going.wait()


def fused_device(
    n_t,
    n_dp,
    tokens,
    clip_ids,
    ln1_gain,
    ln1_bias,
    query_key_value_weight,
    projection_weight,
    attention_output_bias,
    ln2_gain,
    ln2_bias,
    up_weight,
    mlp_up_bias,
    down_weight,
    mlp_down_bias,
    grad_output,
):
    _, rows, width = tokens.shape
    heads_w = projection_weight.shape[0]
    hidden_w = up_weight.shape[1]
    n_y, n_x, n_l, n_h = n_t // CORES, WIDE, PAIR, n_dp // (WIDE * PAIR)
    part = width // n_dp
    blocks = rows // BLOCK
    qkv_w = 3 * heads_w
    def chunk(tag, w):
        sizes = {"h": n_h, "l": n_l, "x": n_x}
        dims, early = ["h", "l", "x"], True
        bufs = [
            pltpu.VMEM((n_t, n_h, n_l, n_x, part, w), BF),
            pltpu.VMEM((n_y, n_h, n_l, n_x, part, w), BF),
        ]
        for step in ORDER[tag]:
            if step == "g":
                bufs.append(pltpu.VMEM((n_y, n_h, part, w), BF))
                break
            if step == "y":
                early = False
                lead = (n_y - 1,)
            else:
                group = AXES[step]
                dims = [a for a in dims if a not in group]
                lead = ((n_y,) if early else ()) + (math.prod(sizes[a] for a in group) - 1,)
            bufs.append(pltpu.VMEM(lead + tuple(sizes[a] for a in dims) + (part, w), BF))
        return bufs

    def half(*shape):
        return pltpu.VMEM(shape, BF)

    def single(*shape):
        return pltpu.VMEM(shape, F32)

    scratch = [
        half(rows, width),
        half(rows, width),
        half(n_t, 3, width, heads_w),
        half(n_t, heads_w, width),
        half(n_t, width, hidden_w),
        half(n_t, hidden_w, width),
        single(n_t, 8, hidden_w),
        half(rows, width),
        single(4, rows, BLOCK),
        half(n_t, rows, heads_w),
        half(n_t, rows + BLOCK, heads_w),
        half(n_t, rows + BLOCK, heads_w),
        half(n_t, heads_w, rows + BLOCK),
        half(n_t, heads_w, rows + BLOCK),
        single(blocks, 2 * BLOCK, BLOCK),
        half(n_t, blocks, 2 * BLOCK, 2 * BLOCK),
        half(rows, n_t * heads_w),
        single(rows, width),
        half(rows, width),
        single(rows, width),
        half(rows, n_t * hidden_w),
        half(CORES, rows, hidden_w),
        half(rows, hidden_w),
        half(rows, width),
        half(rows, n_t * heads_w),
        half(rows, n_t * qkv_w),
        single(6, 8, width),
        single(n_t, 8, hidden_w),
        single(n_t, 8, width),
        single(n_t - 1, 8, width),
        single(8, width),
        single(n_dp - 1, 8, BLOCK),
        chunk("u", hidden_w),
        chunk("d", hidden_w),
        chunk("qk", 2 * heads_w),
        chunk("pv", 2 * heads_w),
        half(rows, width),
        half(rows, width),
        pltpu.SemaphoreType.DMA((8,)),
        pltpu.SemaphoreType.DMA((128,)),
        pltpu.SemaphoreType.DMA((128,)),
    ]
    anywhere = pl.BlockSpec(memory_space=pl.ANY)
    near = pl.BlockSpec(memory_space=pltpu.VMEM)
    results = pl.pallas_call(
        functools.partial(layer_kernel, (n_t, n_dp, rows, width, heads_w, hidden_w)),
        out_shape=(
            jax.ShapeDtypeStruct((rows, width), BF),
            jax.ShapeDtypeStruct((rows, width), BF),
            jax.ShapeDtypeStruct((3, part, heads_w), F32),
            jax.ShapeDtypeStruct((part, heads_w), F32),
            jax.ShapeDtypeStruct((part, hidden_w), F32),
            jax.ShapeDtypeStruct((part, hidden_w), F32),
            jax.ShapeDtypeStruct((8, BLOCK), F32),
        ),
        in_specs=[anywhere] * 2 + [near] * 8 + [anywhere] * 4,
        out_specs=[anywhere] * 2 + [near] * 5,
        scratch_shapes=scratch,
        compiler_params=pltpu.CompilerParams(
            collective_id=0, has_side_effects=True, vmem_limit_bytes=63 << 20
        ),
    )(
        tokens.reshape(rows, width),
        grad_output.reshape(rows, width),
        clip_ids,
        ln1_gain.reshape(1, width),
        ln1_bias.reshape(1, width),
        attention_output_bias.reshape(1, width),
        ln2_gain.reshape(1, width),
        ln2_bias.reshape(1, width),
        mlp_down_bias.reshape(1, width),
        mlp_up_bias.reshape(1, hidden_w),
        jnp.transpose(query_key_value_weight, (1, 0, 2)),
        projection_weight,
        up_weight,
        down_weight,
    )
    share = width // (n_dp * n_t)
    out, gtok, gq, gp, gu, gd, *vectors, g_up_bias = pl.pallas_call(
        functools.partial(result_kernel, (n_t, n_dp, width)),
        out_shape=[jax.ShapeDtypeStruct(r.shape, r.dtype) for r in results[:6]]
        + [jax.ShapeDtypeStruct((1, share), F32)] * 6
        + [jax.ShapeDtypeStruct((1, hidden_w // n_dp), F32)],
        in_specs=[anywhere] * 6 + [near],
        out_specs=[anywhere] * 6 + [near] * 7,
        scratch_shapes=[pltpu.VMEM(r.shape, r.dtype) for r in results[:6]]
        + [pltpu.SemaphoreType.DMA((6 * PARTS,))] * 2,
        compiler_params=pltpu.CompilerParams(vmem_limit_bytes=63 << 20),
    )(*results)
    vectors = [v.reshape(share) for v in vectors]
    return (
        out[None],
        gtok[None],
        vectors[0],
        vectors[1],
        jnp.transpose(gq, (1, 0, 2)),
        gp.T,
        vectors[2],
        vectors[3],
        vectors[4],
        gu,
        g_up_bias,
        gd.T,
        vectors[5],
    )


def fits(mesh, shapes):
    n_t, n_dp = mesh.shape["tensor"], mesh.shape["dp"]
    seqs, length, width = shapes[0]
    features = shapes[4][2] // n_t
    hidden_w = shapes[9][1] // n_t
    return (
        seqs == n_t * n_dp
        and length % ROWS == 0
        and features == 2 * HD == BLOCK
        and hidden_w == width
        and n_t % CORES == 0
        and n_t // CORES > 1
        and n_dp % (2 * WIDE) == 0
        and (width // n_dp) % 16 == 0
    )


def solution(mesh):
    in_specs = (
        P(("dp", "tensor"), None, None),
        P("dp", None),
        P(),
        P(),
        P(None, None, "tensor"),
        P("tensor", None),
        P(),
        P(),
        P(),
        P(None, "tensor"),
        P("tensor"),
        P("tensor", None),
        P(),
        P(("dp", "tensor"), None, None),
    )
    out_specs = (
        P(("dp", "tensor"), None, None),
        P(("dp", "tensor"), None, None),
        P(("dp", "tensor")),
        P(("dp", "tensor")),
        P("dp", None, "tensor"),
        P("tensor", "dp"),
        P(("dp", "tensor")),
        P(("dp", "tensor")),
        P(("dp", "tensor")),
        P("dp", "tensor"),
        P("tensor", "dp"),
        P("tensor", "dp"),
        P(("dp", "tensor")),
    )

    def run(*arrays):
        body = on_device
        if fits(mesh, [a.shape for a in arrays]):
            body = functools.partial(fused_device, mesh.shape["tensor"], mesh.shape["dp"])
        return jax.shard_map(
            body, mesh=mesh, in_specs=in_specs, out_specs=out_specs, check_vma=False
        )(*arrays)

    return run
```

```python
import functools
import math

import jax
import jax.numpy as jnp
from jax import lax
from jax.experimental import pallas as pl
from jax.experimental.pallas import tpu as pltpu
from jax.sharding import PartitionSpec as P

HD = 64
CORES = 2
WIDE = 2
PAIR = 2
BF = jnp.bfloat16
F32 = jnp.float32
MESH = pl.DeviceIdType.MESH


epsilon = 1e-05


def layer_norm(values, gain, shift):
    centre = values - jnp.mean(values, axis=-1, keepdims=True)
    spread = jnp.mean(centre * centre, axis=-1, keepdims=True)
    return centre * lax.rsqrt(spread + epsilon) * gain + shift


def gelu_exact(values):
    return jax.nn.gelu(values, approximate=False)


def visible(clip_row, start, count):
    length = clip_row.shape[0]
    query_pos = start + jnp.arange(count)
    key_pos = jnp.arange(length)
    query_clip = clip_row[start : start + count]
    return (key_pos[None, :] <= query_pos[:, None]) & (query_clip[:, None] == clip_row[None, :])


def block_scores(query, keys, clip_row, start, block):
    scale = query.shape[-1] ** (-0.5)
    allowed = visible(clip_row, start, block)
    scores = (
        jnp.einsum(
            "qhd,khd->hqk", query[start : start + block], keys, preferred_element_type=jnp.float32
        )
        * scale
    )
    return (jnp.where(allowed[None], scores, -1e30), allowed)


def attend_sequence(pieces):
    query, keys, vals, clip_row = pieces
    length = query.shape[0]
    block = min(512, length)
    outs = []
    sums = []
    for start in range(0, length, block):
        scores, allowed = block_scores(query, keys, clip_row, start, block)
        peak = jnp.max(scores, axis=-1, keepdims=True)
        expo = jnp.exp(scores - peak)
        total = jnp.sum(expo, axis=-1, keepdims=True)
        probs = (expo / total).astype(jnp.bfloat16)
        outs.append(jnp.einsum("hqk,khd->qhd", probs, vals, preferred_element_type=jnp.float32))
        sums.append((peak + jnp.log(total))[..., 0])
    return (jnp.concatenate(outs, 0), jnp.concatenate(sums, 1))


def attend_back(pieces):
    query, keys, vals, clip_row, lse, grad_mixed = pieces
    length = query.shape[0]
    block = min(512, length)
    scale = query.shape[-1] ** (-0.5)
    grad_keys = jnp.zeros(keys.shape, jnp.float32)
    grad_vals = jnp.zeros(vals.shape, jnp.float32)
    query_parts = []
    for start in range(0, length, block):
        scores, allowed = block_scores(query, keys, clip_row, start, block)
        probs_f = jnp.where(
            allowed[None], jnp.exp(scores - lse[:, start : start + block, None]), 0.0
        )
        probs = probs_f.astype(jnp.bfloat16)
        grad_block = grad_mixed[start : start + block]
        dprobs = jnp.einsum("qhd,khd->hqk", grad_block, vals, preferred_element_type=jnp.float32)
        grad_vals = grad_vals + jnp.einsum(
            "hqk,qhd->khd", probs, grad_block, preferred_element_type=jnp.float32
        )
        inner = jnp.sum(probs_f * dprobs, axis=-1, keepdims=True)
        dscores = (probs_f * (dprobs - inner)).astype(jnp.bfloat16)
        query_parts.append(
            jnp.einsum("hqk,khd->qhd", dscores, keys, preferred_element_type=jnp.float32) * scale
        )
        grad_keys = (
            grad_keys
            + jnp.einsum(
                "hqk,qhd->khd",
                dscores,
                query[start : start + block],
                preferred_element_type=jnp.float32,
            )
            * scale
        )
    return (jnp.concatenate(query_parts, 0), grad_keys, grad_vals)


def on_device(
    tokens,
    clip_ids,
    ln1_gain,
    ln1_bias,
    query_key_value_weight,
    projection_weight,
    attention_output_bias,
    ln2_gain,
    ln2_bias,
    up_weight,
    mlp_up_bias,
    down_weight,
    mlp_down_bias,
    grad_output,
):
    head_size = HD
    local_width = query_key_value_weight.shape[2]
    local_heads = local_width // head_size
    tok_f = tokens.astype(jnp.float32)
    first_normalized = layer_norm(tok_f, ln1_gain, ln1_bias).astype(jnp.bfloat16)
    first_normalized_every = lax.all_gather(first_normalized, "tensor", axis=0, tiled=True)
    seqs = first_normalized_every.shape[0]
    length = first_normalized_every.shape[1]
    query_key_value_rows = jnp.einsum(
        "tre,eub->trub",
        first_normalized_every,
        query_key_value_weight,
        preferred_element_type=jnp.float32,
    ).astype(jnp.bfloat16)
    query_key_value_rows = query_key_value_rows.reshape(seqs, length, 3, local_heads, head_size)
    query = query_key_value_rows[:, :, 0]
    keys = query_key_value_rows[:, :, 1]
    vals = query_key_value_rows[:, :, 2]
    mixed_heads_output, lse = lax.map(attend_sequence, (query, keys, vals, clip_ids))
    mixed_heads_lowered = mixed_heads_output.astype(jnp.bfloat16).reshape(seqs, length, local_width)
    attention_piece = jnp.einsum(
        "bne,eo->bno", mixed_heads_lowered, projection_weight, preferred_element_type=jnp.float32
    )
    attn_rows = lax.psum_scatter(
        attention_piece.astype(jnp.bfloat16), "tensor", scatter_dimension=0, tiled=True
    ).astype(jnp.float32)
    hidden_activation = tok_f + attn_rows + attention_output_bias
    second_normalized = layer_norm(hidden_activation, ln2_gain, ln2_bias).astype(jnp.bfloat16)
    second_normalized_every = lax.all_gather(second_normalized, "tensor", axis=0, tiled=True)
    upper_half_rows = (
        jnp.einsum(
            "wih,hm->wim", second_normalized_every, up_weight, preferred_element_type=jnp.float32
        )
        + mlp_up_bias
    )
    active_rows_now = gelu_exact(upper_half_rows).astype(jnp.bfloat16)
    perceptron_piece = jnp.einsum(
        "bne,eo->bno", active_rows_now, down_weight, preferred_element_type=jnp.float32
    )
    mlp_rows = lax.psum_scatter(
        perceptron_piece.astype(jnp.bfloat16), "tensor", scatter_dimension=0, tiled=True
    ).astype(jnp.float32)
    output = (hidden_activation + mlp_rows + mlp_down_bias).astype(jnp.bfloat16)
    gradient_every_row = lax.all_gather(grad_output, "tensor", axis=0, tiled=True)
    down_weight_gradient = jnp.einsum(
        "egz,egb->zb", active_rows_now, gradient_every_row, preferred_element_type=jnp.float32
    )
    gradient_active_rows = jnp.einsum(
        "etk,ok->eto", gradient_every_row, down_weight, preferred_element_type=jnp.float32
    )
    gradient_upper_half = jax.vjp(gelu_exact, upper_half_rows)[1](gradient_active_rows)[0].astype(
        jnp.bfloat16
    )
    g_up_bias = jnp.sum(gradient_upper_half, axis=(0, 1), dtype=jnp.float32)
    up_weight_gradient = jnp.einsum(
        "kjy,kjt->yt",
        second_normalized_every,
        gradient_upper_half,
        preferred_element_type=jnp.float32,
    )
    grad_normed2_part = jnp.einsum(
        "hwm,bm->hwb", gradient_upper_half, up_weight, preferred_element_type=jnp.float32
    )
    grad_normed2 = lax.psum_scatter(
        grad_normed2_part.astype(jnp.bfloat16), "tensor", scatter_dimension=0, tiled=True
    ).astype(jnp.float32)
    grad_hidden_ln, g_ln2_gain, g_ln2_bias = jax.vjp(
        layer_norm, hidden_activation, ln2_gain, ln2_bias
    )[1](grad_normed2)
    grad_f = grad_output.astype(jnp.float32)
    grad_hidden = grad_f + grad_hidden_ln
    g_down_bias = jnp.sum(grad_f, axis=(0, 1))
    g_proj_bias = jnp.sum(grad_hidden, axis=(0, 1))
    branch_low = grad_hidden.astype(jnp.bfloat16)
    branch_every_row = lax.all_gather(branch_low, "tensor", axis=0, tiled=True)
    projection_weight_gradient = jnp.einsum(
        "egz,egb->zb", mixed_heads_lowered, branch_every_row, preferred_element_type=jnp.float32
    )
    grad_mixed = jnp.einsum(
        "etk,ok->eto", branch_every_row, projection_weight, preferred_element_type=jnp.float32
    ).astype(jnp.bfloat16)
    grad_mixed = grad_mixed.reshape(seqs, length, local_heads, head_size)
    grad_query, grad_keys, grad_vals = lax.map(
        attend_back, (query, keys, vals, clip_ids, lse, grad_mixed)
    )
    gradient_query_key_value = (
        jnp.stack((grad_query, grad_keys, grad_vals), axis=2)
        .astype(jnp.bfloat16)
        .reshape(seqs, length, 3, local_width)
    )
    query_key_value_gradient = jnp.einsum(
        "zny,znqj->yqj",
        first_normalized_every,
        gradient_query_key_value,
        preferred_element_type=jnp.float32,
    )
    grad_normed_part = jnp.einsum(
        "kegu,hgu->keh",
        gradient_query_key_value,
        query_key_value_weight,
        preferred_element_type=jnp.float32,
    )
    grad_normed = lax.psum_scatter(
        grad_normed_part.astype(jnp.bfloat16), "tensor", scatter_dimension=0, tiled=True
    ).astype(jnp.float32)
    grad_tok_ln, g_ln1_gain, g_ln1_bias = jax.vjp(layer_norm, tok_f, ln1_gain, ln1_bias)[1](
        grad_normed
    )
    grad_tokens = (grad_hidden + grad_tok_ln).astype(jnp.bfloat16)
    g_qkv_s, g_proj_s, g_up_s, g_up_bias_s, g_down_s = (
        lax.psum_scatter(
            query_key_value_gradient.astype(jnp.bfloat16), "dp", scatter_dimension=0, tiled=True
        ).astype(jnp.float32),
        lax.psum_scatter(
            projection_weight_gradient.astype(jnp.bfloat16), "dp", scatter_dimension=1, tiled=True
        ).astype(jnp.float32),
        lax.psum_scatter(
            up_weight_gradient.astype(jnp.bfloat16), "dp", scatter_dimension=0, tiled=True
        ).astype(jnp.float32),
        lax.psum_scatter(
            g_up_bias[None].astype(jnp.bfloat16), "dp", scatter_dimension=1, tiled=True
        ).astype(jnp.float32),
        lax.psum_scatter(
            down_weight_gradient.astype(jnp.bfloat16), "dp", scatter_dimension=1, tiled=True
        ).astype(jnp.float32),
    )
    v_ln1_gain, v_ln1_bias, v_proj_bias, v_ln2_gain, v_ln2_bias, v_down_bias = (
        lax.psum_scatter(g_ln1_gain, ("dp", "tensor"), scatter_dimension=0, tiled=True),
        lax.psum_scatter(g_ln1_bias, ("dp", "tensor"), scatter_dimension=0, tiled=True),
        lax.psum_scatter(g_proj_bias, ("dp", "tensor"), scatter_dimension=0, tiled=True),
        lax.psum_scatter(g_ln2_gain, ("dp", "tensor"), scatter_dimension=0, tiled=True),
        lax.psum_scatter(g_ln2_bias, ("dp", "tensor"), scatter_dimension=0, tiled=True),
        lax.psum_scatter(g_down_bias, ("dp", "tensor"), scatter_dimension=0, tiled=True),
    )
    return (
        output,
        grad_tokens,
        v_ln1_gain,
        v_ln1_bias,
        g_qkv_s,
        g_proj_s,
        v_proj_bias,
        v_ln2_gain,
        v_ln2_bias,
        g_up_s,
        g_up_bias_s,
        g_down_s,
        v_down_bias,
    )


BLOCK = 128
ROWS = 256
WIDE_ROWS = 512
PARTS = 4
AXES = {"x": ("x",), "l": ("l",), "h": ("h",), "w": ("l", "x"), "z": ("h", "l")}
SOON = ("wq",)

ORDER = {"u": "xlg", "d": "lxg", "qk": "xlg", "pv": "ywh"}
SCHEDULE = {
    "start": ("wp", "wq", "wd",),
    "heads0": ("wu", "wq",),
    "attend1": ("wp", "wq", "wq",),
    "dact": ("wp", "wd",),
    "attend2": ("wp", "wu",),
    "hidden": ("wd",),
    "rows1.1": ("wu",),
    "mlp1": ("d0", "u0",),
    "rows0.0": ("wd",),
    "rows0.1": ("wu",),
    "mlp0": ("u0", "d0",),
    "mlp3": ("u1", "d1",),
    "mlp2": ("u1", "u0", "d1",),
    "qkv3": ("pv1", "qk1", "d0",),
    "qkv2": ("pv1", "qk1", "u1", "u0",),
    "qkv1": ("d1", "qk0", "d0", "pv0",),
    "qkv0": ("qk1", "qk0", "u1",),
    "norm1.0": ("pv0", "pv",),
    "norm1.1": ("vec", "d1",),
    "out.0": ("qk0", "qk1",),
    "out.1": ("vec", "pv", "qk0",),
    "end": ("u", "pv", "vec", "d", "qk",),
}


def mm(left, right):
    return lax.dot_general(left, right, (((1,), (0,)), ((), ())), preferred_element_type=F32)


def mm_nt(left, right):
    return lax.dot_general(left, right, (((1,), (1,)), ((), ())), preferred_element_type=F32)


def mm_tn(left, right):
    return lax.dot_general(left, right, (((0,), (0,)), ((), ())), preferred_element_type=F32)


def normal_parts(u):
    cdf = 0.5 + 0.5 * lax.erf(u * math.sqrt(0.5))
    bell = jnp.exp2(u * u * (-0.5 * math.log2(math.e)))
    return cdf, u * bell * (1.0 / math.sqrt(2.0 * math.pi))


def by_eight(values):
    return jnp.sum(values.reshape(-1, 8, values.shape[-1]), axis=0)


class Copies:
    def __init__(self, send, recv):
        self.send, self.recv, self.made, self.started = send, recv, {}, []

    def describe(self, name, src, dst, device):
        at = self.made.setdefault(name, len(self.made))
        return pltpu.make_async_remote_copy(
            src_ref=src,
            dst_ref=dst,
            send_sem=self.send.at[at],
            recv_sem=self.recv.at[at],
            device_id=device,
            device_id_type=MESH,
        )

    def start(self, name, src, dst, device):
        copy = self.describe(name, src, dst, device)
        copy.start()
        self.started.append(copy)

    def arrived(self, name, dst, device):
        self.describe(name, dst, dst, device).wait_recv()

    def drain(self):
        for copy in self.started:
            copy.wait_send()


def layer_kernel(
    sizes,
    tok_h,
    dy_h,
    clip_ref,
    ln1_gain_ref,
    ln1_bias_ref,
    proj_bias_ref,
    ln2_gain_ref,
    ln2_bias_ref,
    down_bias_ref,
    bu_ref,
    wq_h,
    wp_h,
    wu_h,
    wd_h,
    out_h,
    gtok_h,
    gq_ref,
    gp_ref,
    gu_ref,
    gd_ref,
    gv_ref,
    tok,
    dy,
    wq,
    wp,
    wu,
    wd,
    bu,
    n1,
    stats,
    qs,
    ks,
    vs,
    ks_t,
    vs_t,
    bias,
    probs,
    mixed,
    hidden,
    n2,
    dn2_acc,
    act,
    dact,
    dup,
    branch,
    dmixed,
    dtri,
    vec_acc,
    bup_acc,
    vec_mine,
    vec_t,
    vec_sum,
    vec_dp,
    u_bufs,
    d_bufs,
    qk_bufs,
    pv_bufs,
    out_b,
    gtok_b,
    local_sem,
    send_sem,
    recv_sem,
):
    n_t, n_dp, rows, width, heads_w, hidden_w = sizes
    n_y, n_x, n_l, n_h = n_t // CORES, WIDE, PAIR, n_dp // (WIDE * PAIR)
    blocks = rows // BLOCK
    part = width // n_dp
    qkv_w = 3 * heads_w
    d, t = lax.axis_index("dp"), lax.axis_index("tensor")
    y, c = t // CORES, lax.rem(t, CORES)
    z, x = d // WIDE, lax.rem(d, WIDE)
    z_far, z_near = z // n_l, lax.rem(z, n_l)

    def t_peer(dy_, dc_):
        return (d, lax.rem(y + dy_, n_y) * CORES + lax.rem(c + dc_, CORES))

    def x_peer(k):
        return (z * WIDE + lax.rem(x + k, n_x), t)

    def dp_peer(h_off, l_off, x_off):
        far, near = lax.rem(z_far + h_off, n_h), lax.rem(z_near + l_off, n_l)
        return ((far * n_l + near) * WIDE + lax.rem(x + x_off, n_x), t)

    def l_peer(k):
        return dp_peer(0, k, 0)

    peers = [t_peer(s // CORES, s % CORES) for s in range(1, n_t)]
    peers += [(lax.rem(d + k, n_dp), t) for k in range(1, n_dp)]
    for k in range(1, n_y):
        for h in range(1, n_h):
            peers.append((dp_peer(h, 0, 0)[0], t_peer(k, 0)[1]))
    core = t_peer(0, 1)

    barrier = pltpu.get_barrier_semaphore()
    for peer in peers:
        pl.semaphore_signal(barrier, inc=1, device_id=peer, device_id_type=MESH)

    def local(src, dst, at):
        copy = pltpu.make_async_copy(src, dst, local_sem.at[at])
        copy.start()
        return copy

    load_tok = local(tok_h, tok, 0)
    load_wq = local(wq_h, wq.at[0], 1)
    load_wp = local(wp_h, wp.at[0], 2)
    load_dy = local(dy_h, dy, 3)
    load_wu = local(wu_h, wu.at[0], 4)
    load_wd = local(wd_h, wd.at[0], 5)
    bu[0] = jnp.broadcast_to(bu_ref[...], bu.shape[1:])

    ln1_gain, ln1_bias = ln1_gain_ref[...], ln1_bias_ref[...]
    proj_bias = proj_bias_ref[...]
    ln2_gain, ln2_bias = ln2_gain_ref[...], ln2_bias_ref[...]
    down_bias = down_bias_ref[...]
    vec_acc[...] = jnp.zeros_like(vec_acc)
    bup_acc[...] = jnp.zeros_like(bup_acc)

    clip = clip_ref[pl.ds(t, 1), :].astype(F32)
    key_at = lax.broadcasted_iota(jnp.int32, (BLOCK, BLOCK), 0)
    query_at = lax.broadcasted_iota(jnp.int32, (BLOCK, BLOCK), 1)
    before = jnp.full((BLOCK, BLOCK), -1.0, F32)
    for i in range(blocks):
        row = clip[:, i * BLOCK : (i + 1) * BLOCK]
        ids = jnp.broadcast_to(row, (BLOCK, BLOCK))
        down = ids.T
        bias[i, 0:BLOCK, :] = jnp.where(before == ids, 0.0, -1e30)
        bias[i, BLOCK:, :] = jnp.where((down == ids) & (key_at <= query_at), 0.0, -1e30)
        before = down

    for s in range(n_t):
        ks[s, 0:BLOCK, :] = jnp.zeros((BLOCK, heads_w), BF)
        vs[s, 0:BLOCK, :] = jnp.zeros((BLOCK, heads_w), BF)
        ks_t[s, :, 0:BLOCK] = jnp.zeros((heads_w, BLOCK), BF)
        vs_t[s, :, 0:BLOCK] = jnp.zeros((heads_w, BLOCK), BF)

    def at(i, size, offset=0):
        return pl.ds(pl.multiple_of(i * size + offset, math.gcd(size, offset) if offset else size), size)

    pl.semaphore_wait(barrier, len(peers))
    copies = Copies(send_sem, recv_sem)

    full = {"wq": (wq_h, wq), "wp": (wp_h, wp), "wu": (wu_h, wu), "wd": (wd_h, wd)}

    def rows_of(ref, which, parts):
        part = ref.shape[-2] // parts
        here = pl.ds(pl.multiple_of(which * part, part), part)
        return ref.at[:, here] if len(ref.shape) == 3 else ref.at[here]

    def gather(name):
        src, dst = full[name]
        quarters, mine = n_x * n_l, x * n_l + z_near
        across, along = lax.rem(x + 1, n_x) * n_l + z_near, x * n_l + lax.rem(z_near + 1, n_l)
        last = lax.rem(x + 1, n_x) * n_l + lax.rem(z_near + 1, n_l)

        def spot(k, which, halves=1, half=0):
            return rows_of(dst.at[CORES * k], which * halves + half, quarters * halves)

        def pass_on(k, n):
            which = (mine, across, along, last)[n]
            there = rows_of(dst.at[CORES * k + 1], which, quarters)
            copies.start((name, "core", k, n), spot(k, which), there, core)

        far = range(1, n_y)
        copies.start((name, "core", 0), src, dst.at[1], core)
        for k in far:
            copies.start(
                (name, "y", k), rows_of(src, mine, quarters), spot(k, mine), t_peer(n_y - k, 0)
            )
        yield
        for k in far:
            copies.arrived((name, "y", k), spot(k, mine), core)
            copies.start((name, "x", k), spot(k, mine), spot(k, mine), x_peer(1))
            copies.start((name, "l", k), spot(k, mine), spot(k, mine), l_peer(1))
            pass_on(k, 0)
        yield
        for k in far:
            copies.arrived((name, "x", k), spot(k, across), core)
            first = spot(k, across, 2, 0)
            copies.start((name, "xl", k), first, first, l_peer(1))
            copies.arrived((name, "l", k), spot(k, along), core)
            second = spot(k, along, 2, 1)
            copies.start((name, "lx", k), second, second, x_peer(1))
            pass_on(k, 1)
            pass_on(k, 2)
        yield
        for k in far:
            copies.arrived((name, "xl", k), spot(k, last, 2, 0), core)
            copies.arrived((name, "lx", k), spot(k, last, 2, 1), core)
            pass_on(k, 3)
        yield

    def gather_soon(name):
        src, dst = full[name]
        parts = 2 * n_x
        far = range(1, n_y)

        def spot(k, which, whole_half=False):
            if whole_half:
                return rows_of(dst.at[k], 1, 2)
            return rows_of(dst.at[k], which, parts)

        copies.start((name, "core", 0), src, dst.at[1], core)
        for k in far:
            peer = t_peer(n_y - k, 0)
            copies.start((name, "y", k), rows_of(src, x, parts), spot(CORES * k, x), peer)
        for k in far:
            peer = t_peer(n_y - k, 0)
            second = spot(CORES * k, 0, True)
            copies.start((name, "yy", k), rows_of(src, 1, 2), second, peer)
        yield
        for k in far:
            got = spot(CORES * k, x)
            copies.arrived((name, "y", k), got, core)
            for j in range(1, n_x):
                copies.start((name, "x", k, j), got, got, x_peer(j))
            copies.start((name, "core", k, 0), got, spot(CORES * k + 1, x), core)
        yield
        for k in far:
            got = spot(CORES * k, 0, True)
            copies.arrived((name, "yy", k), got, core)
            copies.start((name, "core", k, n_x), got, spot(CORES * k + 1, 0, True), core)
        yield
        for k in far:
            for j in range(1, n_x):
                which = lax.rem(x + n_x - j, n_x)
                got = spot(CORES * k, which)
                copies.arrived((name, "x", k, j), got, core)
                copies.start((name, "core", k, j), got, spot(CORES * k + 1, which), core)
        yield

    def whole(name, s):
        _, dst = full[name]
        quarters = n_x * n_l
        if s == 1:
            copies.arrived((name, "core", 0), dst.at[1], core)
        elif s % CORES == 1 and name in SOON:
            for j in range(n_x):
                got = rows_of(dst.at[s], lax.rem(x + n_x - j, n_x), 2 * n_x)
                copies.arrived((name, "core", s // CORES, j), got, core)
            copies.arrived((name, "core", s // CORES, n_x), rows_of(dst.at[s], 1, 2), core)
        elif s % CORES == 1:
            here, there = lax.rem(x + 1, n_x) * n_l, lax.rem(z_near + 1, n_l)
            spots = [x * n_l + z_near, here + z_near, x * n_l + there, here + there]
            for n, which in enumerate(spots):
                got = rows_of(dst.at[s], which, quarters)
                copies.arrived((name, "core", s // CORES, n), got, core)

    position = {"x": x, "l": z_near, "h": z_far}
    extent = {"x": n_x, "l": n_l, "h": n_h}
    reduced = {}

    def steps_along(group):
        offsets = [{}]
        for axis in group:
            offsets = [dict(o, **{axis: k}) for o in offsets for k in range(extent[axis])]
        return [o for o in offsets if any(o.values())]

    def part_for(dims, group, offset):
        return tuple(
            lax.rem(position[a] + offset[a], extent[a]) if a in group else slice(None) for a in dims
        )

    def spots_of(dims):
        spots = [()]
        for axis in dims:
            spots = [spot + (a,) for spot in spots for a in range(extent[axis])]
        return spots

    def sum_f32(values):
        return functools.reduce(lambda a, b: a + b, [v.astype(F32) for v in values])

    def send_parts(name, cur, dims, step, recv):
        group = AXES[step]
        for j, offset in enumerate(steps_along(group)):
            peer = dp_peer(*(offset.get(a, 0) for a in ("h", "l", "x")))
            copies.start(
                (name, step, j), cur.at[part_for(dims, group, offset)], recv.at[j], peer
            )

    def fold(name, cur, dims, step, recv, keep=True):
        group = AXES[step]
        others = len(steps_along(group))
        for j in range(others):
            copies.arrived((name, step, j), recv.at[j], core)
        rest = [a for a in dims if a not in group]
        total = None
        for spot in spots_of(rest):
            at_rest = dict(zip(rest, spot))
            mine = cur[tuple(position[a] if a in group else at_rest[a] for a in dims)]
            total = sum_f32([mine] + [recv[(j,) + spot] for j in range(others)])
            if keep:
                recv[(0,) + spot] = total.astype(BF)
        return (recv.at[0] if keep else total), rest

    def reduce_pair(tag, bufs, k):
        order = ORDER[tag]
        at_y = max(order.find("y"), order.find("g"))
        own, got = bufs[:2]
        copies.start((tag, "core", k), own.at[CORES * k + 1], got.at[k], core)
        yield
        copies.arrived((tag, "core", k), got.at[k], core)
        for spot in spots_of(["h", "l", "x"]):
            here = (CORES * k,) + spot
            own[here] = own[here] + got[(k,) + spot]
        cur, dims = own.at[CORES * k], ["h", "l", "x"]
        for n, step in enumerate(order[: at_y]):
            recv = bufs[2 + n].at[k]
            send_parts((tag, k), cur, dims, step, recv)
            yield
            cur, dims = fold((tag, k), cur, dims, step, recv)
        if order[at_y] == "g":
            recv = bufs[-1]
            for off in range(n_h):
                if k or off:
                    mine = cur.at[part_for(dims, ("h",), {"h": off})]
                    peer = (dp_peer(off, 0, 0)[0], t_peer(k, 0)[1])
                    copies.start((tag, "g", k, off), mine, recv.at[k, off], peer)
        elif k > 0:
            copies.start((tag, "y", k), cur, bufs[2 + at_y].at[k - 1], t_peer(k, 0))
        reduced[tag, k] = cur, dims
        yield

    def reduce_end(tag, bufs, write):
        order = ORDER[tag]
        cur, dims = reduced[tag, 0]
        at_y = order.find("y")
        if at_y < 0:
            terms = [cur[z_far]]
            for k in range(n_y):
                for off in range(n_h):
                    if k or off:
                        copies.arrived((tag, "g", k, off), bufs[-1].at[k, off], core)
                        terms.append(bufs[-1][k, off])
            write(sum_f32(terms))
            yield
            return
        recv = bufs[2 + at_y]
        for k in range(1, n_y):
            copies.arrived((tag, "y", k), recv.at[k - 1], core)
        total = None
        for spot in spots_of(dims):
            total = sum_f32([cur[spot]] + [recv[(k,) + spot] for k in range(n_y - 1)])
            if dims:
                recv[(0,) + spot] = total.astype(BF)
        cur = recv.at[0]
        for n, step in enumerate(order[at_y + 1 :]):
            recv = bufs[3 + at_y + n]
            send_parts(tag, cur, dims, step, recv)
            yield
            cur, dims = fold(tag, cur, dims, step, recv, at_y + 2 + n < len(order))
            total = cur
        write(total)
        yield

    def write_up(total):
        gu_ref[...] = total

    def write_down(total):
        gd_ref[...] = total

    def write_query_key(total):
        gq_ref[0] = total[:, :heads_w]
        gq_ref[1] = total[:, heads_w:]

    def write_proj_value(total):
        gp_ref[...] = total[:, :heads_w]
        gq_ref[2] = total[:, heads_w:]

    def lanes_of(who):
        return pl.ds(pl.multiple_of(who * (width // n_dp) // BLOCK * BLOCK, BLOCK), BLOCK)

    def vectors():
        for s in range(n_t):
            lines = [jnp.sum(vec_acc[k], axis=0, keepdims=True) for k in range(6)]
            lines.append(jnp.sum(bup_acc[s], axis=0, keepdims=True))
            lines.append(jnp.zeros((1, width), F32))
            vec_mine[s] = jnp.concatenate(lines, axis=0)
        for s in range(1, n_t):
            copies.start(("vt", s), vec_mine.at[s], vec_t.at[s - 1], t_peer(s // CORES, s % CORES))
        yield
        total = vec_mine[0]
        for s in range(1, n_t):
            copies.arrived(("vt", s), vec_t.at[s - 1], core)
            total = total + vec_t[s - 1]
        vec_sum[...] = total
        for k in range(1, n_dp):
            peer = lax.rem(d + k, n_dp)
            copies.start(("vd", k), vec_sum.at[:, lanes_of(peer)], vec_dp.at[k - 1], (peer, t))
        yield
        total = vec_sum[:, lanes_of(d)]
        for k in range(1, n_dp):
            copies.arrived(("vd", k), vec_dp.at[k - 1], core)
            total = total + vec_dp[k - 1]
        gv_ref[...] = total
        yield

    u_own, d_own, qk_own, pv_own = u_bufs[0], d_bufs[0], qk_bufs[0], pv_bufs[0]
    sums = {
        "u": (u_bufs, write_up),
        "d": (d_bufs, write_down),
        "qk": (qk_bufs, write_query_key),
        "pv": (pv_bufs, write_proj_value),
    }
    steps = {name: gather_soon(name) if name in SOON else gather(name) for name in full}
    for tag, (bufs, write) in sums.items():
        for k in range(n_y):
            steps[tag + str(k)] = reduce_pair(tag, bufs, k)
        steps[tag] = reduce_end(tag, bufs, write)
    steps["vec"] = vectors()

    def tick(name):
        for step in SCHEDULE.get(name, ()):
            next(steps[step])

    tick("start")
    for s in range(1, n_t):
        copies.start(
            ("bu", s),
            bu.at[0],
            bu.at[s],
            t_peer((n_y - s // CORES) % n_y, (CORES - s % CORES) % CORES),
        )

    load_tok.wait()

    @pl.loop(0, rows // ROWS)
    def _(i):
        here = at(i, ROWS)
        v = tok[here, :].astype(F32)
        mean = jnp.mean(v, axis=-1, keepdims=True)
        centre = v - mean
        r = lax.rsqrt(jnp.mean(centre * centre, axis=-1, keepdims=True) + epsilon)
        normed = (centre * r * ln1_gain + ln1_bias).astype(BF)
        n1[here, :] = normed
        stats[0, here, :] = jnp.broadcast_to(mean, (ROWS, BLOCK))
        stats[1, here, :] = jnp.broadcast_to(r, (ROWS, BLOCK))

    first_head = lax.broadcasted_iota(jnp.int32, (BLOCK, heads_w), 1) < HD

    def two_heads(block):
        zero = jnp.zeros_like(block)
        return jnp.concatenate(
            [jnp.where(first_head, block, zero), jnp.where(first_head, zero, block)], axis=0
        )

    def pick_heads(both):
        own = jnp.concatenate([both[:HD, :BLOCK], both[HD:, BLOCK:]], axis=0)
        return own.T

    def qkv_weight(slots):
        return jnp.concatenate([wq[s, j] for s in slots for j in range(3)], axis=1)

    def project_heads(slots):
        @pl.loop(0, rows // WIDE_ROWS)
        def _(i):
            here = at(i, WIDE_ROWS)
            there = at(i, WIDE_ROWS, BLOCK)
            all_of = mm(n1[here, :], qkv_weight(slots)).astype(BF)
            for n, s in enumerate(slots):
                got = all_of[:, n * qkv_w : (n + 1) * qkv_w]
                qs[s, here, :] = got[:, :heads_w] * jnp.asarray(HD**-0.5, BF)
                k = got[:, heads_w : 2 * heads_w]
                v = got[:, 2 * heads_w :]
                ks[s, there, :] = k
                vs[s, there, :] = v
                ks_t[s, :, there] = k.T
                vs_t[s, :, there] = v.T

    heres = [pl.ds(i * BLOCK, BLOCK) for i in range(blocks)]
    seens = [pl.ds(i * BLOCK, 2 * BLOCK) for i in range(blocks)]

    def attend_slot(s):
        scores = [
            mm_nt(ks[s, seen, :], two_heads(qs[s, here, :])) for here, seen in zip(heres, seens)
        ]
        lows = []
        for i in range(blocks):
            one = bias[i]
            score = scores[i] + jnp.concatenate([one, one], axis=1)
            expo = jnp.exp(score - jnp.max(score, axis=0, keepdims=True))
            total = jnp.sum(expo, axis=0, keepdims=True)
            low = (expo * (1.0 / total)).astype(BF)
            probs[s, i] = low
            lows.append(low)
        both = [mm(vs_t[s, :, seen], low) for seen, low in zip(seens, lows)]
        for i in range(blocks):
            mixed[heres[i], s * heads_w : (s + 1) * heads_w] = pick_heads(both[i]).astype(BF)

    load_wq.wait()
    whole("wq", 1)
    project_heads((0, 1))
    tick("heads0")
    attend_slot(0)
    tick("attend0")
    attend_slot(1)
    tick("attend1")
    load_dy.wait()
    load_wd.wait()
    dact[0] = mm_nt(dy[...], wd[0]).astype(BF)
    whole("wd", 1)
    dact[1] = mm_nt(dy[...], wd[1]).astype(BF)
    tick("dact")
    for k in range(1, n_y):
        slots = (CORES * k, CORES * k + 1)
        whole("wq", slots[0])
        whole("wq", slots[1])
        project_heads(slots)
        tick(f"heads{slots[0]}")
        for s in slots:
            attend_slot(s)
            tick(f"attend{s}")

    load_wp.wait()
    for s in range(1, n_t):
        whole("wp", s)

    @pl.loop(0, rows // ROWS)
    def _(i):
        here = at(i, ROWS)
        v = tok[here, :].astype(F32) + proj_bias
        v = v + mm(mixed[here, :], wp[...].reshape(n_t * heads_w, width))
        hidden[here, :] = v
        mean = jnp.mean(v, axis=-1, keepdims=True)
        centre = v - mean
        r = lax.rsqrt(jnp.mean(centre * centre, axis=-1, keepdims=True) + epsilon)
        normed = (centre * r * ln2_gain + ln2_bias).astype(BF)
        n2[here, :] = normed
        stats[2, here, :] = jnp.broadcast_to(mean, (ROWS, BLOCK))
        stats[3, here, :] = jnp.broadcast_to(r, (ROWS, BLOCK))

    tick("hidden")

    def mlp_slot(s, new):
        lanes = slice(s * hidden_w, (s + 1) * hidden_w)
        for i in range(rows // WIDE_ROWS):
            here = pl.ds(i * WIDE_ROWS, WIDE_ROWS)
            u = mm(n2[here, :], wu[s]) + bu[s, 0:1, :]
            back = dact[s, here, :] if s < CORES else mm_nt(dy[here, :], wd[s])
            cdf, bell = normal_parts(u)
            act[here, lanes] = (u * cdf).astype(BF)
            du = (back * (cdf + bell)).astype(BF)
            dup[here, :] = du
            bup_acc[s] += by_eight(du.astype(F32))
            back_part = mm_nt(du, wu[s])
            if new:
                dn2_acc[here, :] = back_part
            else:
                dn2_acc[here, :] += back_part
            tick(f"rows{s}.{i}")
        split = (n_h, n_l, n_x, part, hidden_w)
        u_own[s] = mm_tn(n2[...], dup[...]).astype(BF).reshape(split)
        d_own[s] = mm_tn(dy[...], act[:, lanes]).astype(BF).reshape(split)
        tick(f"mlp{s}")

    load_wu.wait()
    for s in range(1, n_t):
        copies.arrived(("bu", s), bu.at[s], core)
    order = [s + 1 - 2 * (s % CORES) for s in range(n_t)]
    for s in order:
        whole("wu", s)
        if s != 1:
            whole("wd", s)
        mlp_slot(s, s == order[0])

    for i in range(rows // WIDE_ROWS):
        here = pl.ds(i * WIDE_ROWS, WIDE_ROWS)
        value = hidden[here, :]
        mean = stats[2, here, 0:1]
        r = stats[3, here, 0:1]
        xhat = (value - mean) * r
        dn = dn2_acc[here, :]
        g = dy[here, :].astype(F32)
        scaled = dn * ln2_gain
        first = jnp.mean(scaled, axis=-1, keepdims=True)
        second = jnp.mean(scaled * xhat, axis=-1, keepdims=True)
        dh = g + r * (scaled - first - xhat * second)
        dn2_acc[here, :] = dh
        low = dh.astype(BF)
        branch[here, :] = low
        dmixed[here, :] = mm_nt(low, wp[...].reshape(n_t * heads_w, width)).astype(BF)
        vec_acc[2] += by_eight(dh)
        vec_acc[3] += by_eight(dn * xhat)
        vec_acc[4] += by_eight(dn)
        vec_acc[5] += by_eight(g)
        tick(f"norm2.{i}")

    got = mm_tn(branch[...], mixed[...]).astype(BF)
    for s in range(n_t):
        pv_own[s, :, :, :, :, :heads_w] = got[:, s * heads_w : (s + 1) * heads_w].reshape(
            n_h, n_l, n_x, part, heads_w
        )
    tick("proj")

    def attend_back_slot(s):
        lanes = slice(s * heads_w, (s + 1) * heads_w)
        first = s * qkv_w
        grads = [two_heads(dmixed[here, lanes]) for here in heres]
        dprobs = [mm_nt(vs[s, seen, :], grad) for seen, grad in zip(seens, grads)]
        ds = []
        for i in range(blocks):
            p = probs[s, i].astype(F32)
            weighed = p * dprobs[i]
            ds.append((weighed - p * jnp.sum(weighed, axis=0, keepdims=True)).astype(BF))
        dv = [mm(probs[s, i], grads[i]) for i in range(blocks)]
        dk = [mm(ds[i], two_heads(qs[s, heres[i], :])) for i in range(blocks)]
        dq = [pick_heads(mm(ks_t[s, :, seens[i]], ds[i])) * (HD**-0.5) for i in range(blocks)]
        for i in range(blocks):
            k_sum, v_sum = dk[i][BLOCK:], dv[i][BLOCK:]
            if i + 1 < blocks:
                k_sum, v_sum = k_sum + dk[i + 1][:BLOCK], v_sum + dv[i + 1][:BLOCK]
            dtri[heres[i], first : first + heads_w] = dq[i].astype(BF)
            dtri[heres[i], first + heads_w : first + 2 * heads_w] = k_sum.astype(BF)
            dtri[heres[i], first + 2 * heads_w : first + qkv_w] = v_sum.astype(BF)
        tick(f"back{s}")
        got = mm_tn(n1[...], dtri[:, first : first + qkv_w]).astype(BF)
        qk_own[s] = got[:, : 2 * heads_w].reshape(n_h, n_l, n_x, part, 2 * heads_w)
        pv_own[s, :, :, :, :, heads_w:] = got[:, 2 * heads_w :].reshape(
            n_h, n_l, n_x, part, heads_w
        )
        tick(f"qkv{s}")

    for s in reversed(range(n_t)):
        attend_back_slot(s)

    for i in range(rows // WIDE_ROWS):
        here = pl.ds(i * WIDE_ROWS, WIDE_ROWS)
        dn = mm_nt(dtri[here, :], qkv_weight(range(n_t)))
        mean = stats[0, here, 0:1]
        r = stats[1, here, 0:1]
        xhat = (tok[here, :].astype(F32) - mean) * r
        scaled = dn * ln1_gain
        first = jnp.mean(scaled, axis=-1, keepdims=True)
        second = jnp.mean(scaled * xhat, axis=-1, keepdims=True)
        gtok_b[here, :] = (dn2_acc[here, :] + r * (scaled - first - xhat * second)).astype(BF)
        vec_acc[0] += by_eight(dn * xhat)
        vec_acc[1] += by_eight(dn)
        tick(f"norm1.{i}")

    store_gtok = local(gtok_b, gtok_h, 7)

    for i in range(rows // WIDE_ROWS):
        here = pl.ds(i * WIDE_ROWS, WIDE_ROWS)
        grown = mm(act[here, :], wd[...].reshape(n_t * hidden_w, width))
        out_b[here, :] = (hidden[here, :] + grown + down_bias).astype(BF)
        tick(f"out.{i}")

    store_out = local(out_b, out_h, 6)

    tick("end")
    store_out.wait()
    store_gtok.wait()
    copies.drain()


def result_kernel(sizes, *refs):
    n_t, n_dp, width = sizes
    sources, vec, results, shares = refs[:6], refs[6], refs[7:13], refs[13:20]
    near, in_sems, out_sems = refs[20:26], refs[26], refs[27]
    pieces = []
    for src, mid, dst in zip(sources, near, results):
        parts = PARTS if src.shape[0] % (PARTS * ROWS) == 0 else 1
        step = src.shape[0] // parts
        for i in range(parts):
            here, at = pl.ds(i * step, step), len(pieces)
            coming = pltpu.make_async_copy(src.at[here], mid.at[here], in_sems.at[at])
            going = pltpu.make_async_copy(mid.at[here], dst.at[here], out_sems.at[at])
            coming.start()
            pieces.append((coming, going))
    for coming, going in pieces:
        coming.wait()
        going.start()
    d, t = lax.axis_index("dp"), lax.axis_index("tensor")
    first = lax.rem(d * (width // n_dp), BLOCK)
    lines = pltpu.roll(vec[...], lax.rem(BLOCK - first, BLOCK), 1)
    shares[6][...] = lines[6:7, : shares[6].shape[1]]
    first = first + t * (width // (n_dp * n_t))
    lines = pltpu.roll(vec[...], lax.rem(BLOCK - first, BLOCK), 1)
    for i in range(6):
        shares[i][...] = lines[i : i + 1, : shares[i].shape[1]]
    for _, going in pieces:
        going.wait()


def fused_device(
    n_t,
    n_dp,
    tokens,
    clip_ids,
    ln1_gain,
    ln1_bias,
    query_key_value_weight,
    projection_weight,
    attention_output_bias,
    ln2_gain,
    ln2_bias,
    up_weight,
    mlp_up_bias,
    down_weight,
    mlp_down_bias,
    grad_output,
):
    _, rows, width = tokens.shape
    heads_w = projection_weight.shape[0]
    hidden_w = up_weight.shape[1]
    n_y, n_x, n_l, n_h = n_t // CORES, WIDE, PAIR, n_dp // (WIDE * PAIR)
    part = width // n_dp
    blocks = rows // BLOCK
    qkv_w = 3 * heads_w
    def chunk(tag, w):
        sizes = {"h": n_h, "l": n_l, "x": n_x}
        dims, early = ["h", "l", "x"], True
        bufs = [
            pltpu.VMEM((n_t, n_h, n_l, n_x, part, w), BF),
            pltpu.VMEM((n_y, n_h, n_l, n_x, part, w), BF),
        ]
        for step in ORDER[tag]:
            if step == "g":
                bufs.append(pltpu.VMEM((n_y, n_h, part, w), BF))
                break
            if step == "y":
                early = False
                lead = (n_y - 1,)
            else:
                group = AXES[step]
                dims = [a for a in dims if a not in group]
                lead = ((n_y,) if early else ()) + (math.prod(sizes[a] for a in group) - 1,)
            bufs.append(pltpu.VMEM(lead + tuple(sizes[a] for a in dims) + (part, w), BF))
        return bufs

    def half(*shape):
        return pltpu.VMEM(shape, BF)

    def single(*shape):
        return pltpu.VMEM(shape, F32)

    scratch = [
        half(rows, width),
        half(rows, width),
        half(n_t, 3, width, heads_w),
        half(n_t, heads_w, width),
        half(n_t, width, hidden_w),
        half(n_t, hidden_w, width),
        single(n_t, 8, hidden_w),
        half(rows, width),
        single(4, rows, BLOCK),
        half(n_t, rows, heads_w),
        half(n_t, rows + BLOCK, heads_w),
        half(n_t, rows + BLOCK, heads_w),
        half(n_t, heads_w, rows + BLOCK),
        half(n_t, heads_w, rows + BLOCK),
        single(blocks, 2 * BLOCK, BLOCK),
        half(n_t, blocks, 2 * BLOCK, 2 * BLOCK),
        half(rows, n_t * heads_w),
        single(rows, width),
        half(rows, width),
        single(rows, width),
        half(rows, n_t * hidden_w),
        half(CORES, rows, hidden_w),
        half(rows, hidden_w),
        half(rows, width),
        half(rows, n_t * heads_w),
        half(rows, n_t * qkv_w),
        single(6, 8, width),
        single(n_t, 8, hidden_w),
        single(n_t, 8, width),
        single(n_t - 1, 8, width),
        single(8, width),
        single(n_dp - 1, 8, BLOCK),
        chunk("u", hidden_w),
        chunk("d", hidden_w),
        chunk("qk", 2 * heads_w),
        chunk("pv", 2 * heads_w),
        half(rows, width),
        half(rows, width),
        pltpu.SemaphoreType.DMA((8,)),
        pltpu.SemaphoreType.DMA((128,)),
        pltpu.SemaphoreType.DMA((128,)),
    ]
    anywhere = pl.BlockSpec(memory_space=pl.ANY)
    near = pl.BlockSpec(memory_space=pltpu.VMEM)
    results = pl.pallas_call(
        functools.partial(layer_kernel, (n_t, n_dp, rows, width, heads_w, hidden_w)),
        out_shape=(
            jax.ShapeDtypeStruct((rows, width), BF),
            jax.ShapeDtypeStruct((rows, width), BF),
            jax.ShapeDtypeStruct((3, part, heads_w), F32),
            jax.ShapeDtypeStruct((part, heads_w), F32),
            jax.ShapeDtypeStruct((part, hidden_w), F32),
            jax.ShapeDtypeStruct((part, hidden_w), F32),
            jax.ShapeDtypeStruct((8, BLOCK), F32),
        ),
        in_specs=[anywhere] * 2 + [near] * 8 + [anywhere] * 4,
        out_specs=[anywhere] * 2 + [near] * 5,
        scratch_shapes=scratch,
        compiler_params=pltpu.CompilerParams(
            collective_id=0, has_side_effects=True, vmem_limit_bytes=63 << 20
        ),
    )(
        tokens.reshape(rows, width),
        grad_output.reshape(rows, width),
        clip_ids,
        ln1_gain.reshape(1, width),
        ln1_bias.reshape(1, width),
        attention_output_bias.reshape(1, width),
        ln2_gain.reshape(1, width),
        ln2_bias.reshape(1, width),
        mlp_down_bias.reshape(1, width),
        mlp_up_bias.reshape(1, hidden_w),
        jnp.transpose(query_key_value_weight, (1, 0, 2)),
        projection_weight,
        up_weight,
        down_weight,
    )
    share = width // (n_dp * n_t)
    out, gtok, gq, gp, gu, gd, *vectors, g_up_bias = pl.pallas_call(
        functools.partial(result_kernel, (n_t, n_dp, width)),
        out_shape=[jax.ShapeDtypeStruct(r.shape, r.dtype) for r in results[:6]]
        + [jax.ShapeDtypeStruct((1, share), F32)] * 6
        + [jax.ShapeDtypeStruct((1, hidden_w // n_dp), F32)],
        in_specs=[anywhere] * 6 + [near],
        out_specs=[anywhere] * 6 + [near] * 7,
        scratch_shapes=[pltpu.VMEM(r.shape, r.dtype) for r in results[:6]]
        + [pltpu.SemaphoreType.DMA((6 * PARTS,))] * 2,
        compiler_params=pltpu.CompilerParams(vmem_limit_bytes=63 << 20),
    )(*results)
    vectors = [v.reshape(share) for v in vectors]
    return (
        out[None],
        gtok[None],
        vectors[0],
        vectors[1],
        jnp.transpose(gq, (1, 0, 2)),
        gp.T,
        vectors[2],
        vectors[3],
        vectors[4],
        gu,
        g_up_bias,
        gd.T,
        vectors[5],
    )


def fits(mesh, shapes):
    n_t, n_dp = mesh.shape["tensor"], mesh.shape["dp"]
    seqs, length, width = shapes[0]
    features = shapes[4][2] // n_t
    hidden_w = shapes[9][1] // n_t
    return (
        seqs == n_t * n_dp
        and length % ROWS == 0
        and features == 2 * HD == BLOCK
        and hidden_w == width
        and n_t % CORES == 0
        and n_t // CORES > 1
        and n_dp % (2 * WIDE) == 0
        and (width // n_dp) % 16 == 0
    )


def solution(mesh):
    in_specs = (
        P(("dp", "tensor"), None, None),
        P("dp", None),
        P(),
        P(),
        P(None, None, "tensor"),
        P("tensor", None),
        P(),
        P(),
        P(),
        P(None, "tensor"),
        P("tensor"),
        P("tensor", None),
        P(),
        P(("dp", "tensor"), None, None),
    )
    out_specs = (
        P(("dp", "tensor"), None, None),
        P(("dp", "tensor"), None, None),
        P(("dp", "tensor")),
        P(("dp", "tensor")),
        P("dp", None, "tensor"),
        P("tensor", "dp"),
        P(("dp", "tensor")),
        P(("dp", "tensor")),
        P(("dp", "tensor")),
        P("dp", "tensor"),
        P("tensor", "dp"),
        P("tensor", "dp"),
        P(("dp", "tensor")),
    )

    def run(*arrays):
        body = on_device
        if fits(mesh, [a.shape for a in arrays]):
            body = functools.partial(fused_device, mesh.shape["tensor"], mesh.shape["dp"])
        return jax.shard_map(
            body, mesh=mesh, in_specs=in_specs, out_specs=out_specs, check_vma=False
        )(*arrays)

    return run
```
